128 devices in a mesh: dp: 32 (over z, x, core), grp: 4 (over y).
Axes of the slice: x: 4, y: 4, z: 4, core: 2. Of those that a mesh axis runs over, the one named last changes fastest.
Arguments:
- features: bfloat16 [16384, 1024], P(('dp', 'grp')), may hold values from -24 to 24
- proj_weight: bfloat16 [1024, 512], replicated, may hold values from -0.01171875 to 0.01171875
- labels: int32 [16384], P(('dp', 'grp')), may hold values from 0 to 511, as said below
- owner_slot: int32 [512], replicated, may hold values from 0 to 511, each once
Outputs:
- projected_grad: bfloat16 [16384, 512], P(('dp', 'grp'))
- weight_grad: float32 [1024, 512], P(('dp', 'grp'))
- owned_sums: float32 [512, 512], P(('dp', 'grp'))
The draws below stay inside these ranges and needn't reach their ends.
Inputs may be any that keep to these rules, and one draw needn't show every extreme that they name: `labels`: every class of 0 to 511 has 1 to 64 rows, some class exactly 64; rows of a class lie anywhere in the batch. `owner_slot`: A permutation.
All inputs are finite; a program needn't handle non-finite values.
Results may differ from the reference program's by a relative error of at most 0.0036.
The reference program's roundings to bfloat16 on the way count: a program that leaves them out, or rounds other values in their place, can miss the bound.
Values may be sent and summed in bfloat16 or wider, within the bound.
A program may use at most 128 MiB of HBM per device.

```python
import jax
import jax.numpy as jnp
from jax import lax

F = 1024
E = 512
TOTAL = 16384
CLASSES = 512


def draw_labels(key, part):
    quads = TOTAL // 128
    key_one, key_two, key_three, key_four = jax.random.split(key, 4)
    first_size = jax.random.randint(key_one, (quads,), 1, 63)
    second_size = jax.random.randint(key_two, (quads,), 1, 64 - first_size)
    position = jnp.arange(128, dtype=jnp.int32)[None, :]
    within = (position >= 64).astype(jnp.int32)
    within = within + (position >= 64 + first_size[:, None]).astype(jnp.int32)
    within = within + (position >= 64 + first_size[:, None] + second_size[:, None]).astype(jnp.int32)
    class_ids = within + 4 * jnp.arange(quads, dtype=jnp.int32)[:, None]
    relabel = jax.random.permutation(key_three, CLASSES).astype(jnp.int32)
    flat = relabel[class_ids.reshape(-1)]
    order = jax.random.permutation(key_four, TOTAL)
    return flat[order].astype(jnp.int32)


def spiked(entries, rng, source, target, blocks, factor):
    owner, partner = [(jnp.arange(entries.shape[axis_at]) // (entries.shape[axis_at] // blocks)).reshape([-1 if axis == axis_at else 1 for axis in range(entries.ndim)]) for axis_at in (source, target)]
    chosen = jax.random.permutation(rng, blocks)[partner]
    strong = (owner == chosen) | (owner == (partner + blocks // 2) % blocks)
    return jnp.where(strong, factor * entries, entries)


def block_levels(stream_key, extent, pieces, least, largest):
    def one(dim, shards_of):
        steps = jax.random.uniform(jax.random.fold_in(jax.random.fold_in(stream_key, 6), dim), (shards_of,), jnp.float32, least / len(pieces), largest / len(pieces))
        return jnp.repeat(jnp.exp(steps), extent[dim] // shards_of).reshape((-1,) + (1,) * (len(extent) - dim - 1))

    level = one(*pieces[0])
    for cut in pieces[1:]:
        level = level * one(*cut)
    return level


def normal_values(own_key, dims, width, bound, pieces=(), kind=jnp.bfloat16):
    factor_of = block_levels(own_key, dims, pieces, -0.22, 0.18) if pieces else 1.0
    result = jax.random.normal(own_key, dims, jnp.float32) * width * factor_of
    return jnp.minimum(jnp.maximum(result, -bound), bound).astype(kind)


def gaussian_with(stream_key, extent, width, reach, shards, heavy, kind=jnp.bfloat16):
    drawn = width * jax.random.normal(stream_key, extent, jnp.float32)
    if shards:
        drawn = drawn * block_levels(stream_key, extent, shards, -0.22, 0.18)
    return jnp.clip(spiked(drawn, jax.random.fold_in(stream_key, 3), *heavy), -reach, reach).astype(kind)


def setup_inputs(seed: int = 0) -> dict:
    key_of = jax.random.split(jax.random.key(seed), 5)
    return {
        "features": gaussian_with(key_of[0], (TOTAL, F), 1.0, 24.0, ((0, 128),), (0, 1, 128, 5.5)),
        "proj_weight": normal_values(key_of[1], (F, E), (256 * F) ** -0.5, 0.01171875),
        "labels": draw_labels(jax.random.fold_in(key_of[4], 71), 0),
        "owner_slot": jax.random.permutation(key_of[3], CLASSES).astype(jnp.int32),
    }


sharpness_divisor = 0.1

def reference(features, proj_weight, labels, owner_slot):
    total_rows = features.shape[0]
    class_total = owner_slot.shape[0]
    projected = jnp.dot(features, proj_weight, preferred_element_type=jnp.float32)
    inv_norm = lax.rsqrt(lax.optimization_barrier(jnp.sum(projected * projected, axis=1, keepdims=True)) + 1e-06)
    unit = projected * inv_norm
    unit_vectors_brain16 = unit.astype(jnp.bfloat16)
    blocks = total_rows // 512
    col_index = jnp.arange(total_rows, dtype=jnp.int32)

    def block_logits(block):
        first_row = (block * 512).astype(jnp.int32)
        part = lax.dynamic_slice_in_dim(unit_vectors_brain16, first_row, 512, 0)
        cosine_score_matrix = lax.dot_general(part, unit_vectors_brain16, (((1,), (1,)), ((), ())), preferred_element_type=jnp.float32) / sharpness_divisor
        self_mask = col_index[None, :] == (first_row + jnp.arange(512, dtype=jnp.int32))[:, None]
        return (cosine_score_matrix, self_mask, first_row)

    def row_total(block):
        cosine_score_matrix, self_mask, first_row = block_logits(block)
        return jnp.log(lax.optimization_barrier(jnp.sum(jnp.where(self_mask, jnp.float32(0.0), jnp.exp(cosine_score_matrix)), axis=1)))
    block_ids = jnp.arange(blocks, dtype=jnp.int32)
    log_total = lax.map(row_total, block_ids).reshape(total_rows)

    def row_grad(block):
        cosine_score_matrix, self_mask, first_row = block_logits(block)
        mine = lax.dynamic_slice_in_dim(log_total, first_row, 512, 0)
        row_prob = jnp.where(self_mask, jnp.float32(0.0), jnp.exp(cosine_score_matrix - mine[:, None])).astype(jnp.bfloat16)
        col_prob = jnp.where(self_mask, jnp.float32(0.0), jnp.exp(cosine_score_matrix - log_total[None, :])).astype(jnp.bfloat16)
        return jnp.dot(row_prob, unit_vectors_brain16, preferred_element_type=jnp.float32) + jnp.dot(col_prob, unit_vectors_brain16, preferred_element_type=jnp.float32)
    anchor_target_share = lax.map(row_grad, block_ids).reshape(total_rows, -1)
    row_slot = owner_slot[labels].astype(jnp.int32)
    slot_hot = row_slot[:, None] == jnp.arange(class_total, dtype=jnp.int32)[None, :]
    owned_sums = lax.dot_general(slot_hot.astype(jnp.bfloat16), unit_vectors_brain16, (((0,), (0,)), ((), ())), preferred_element_type=jnp.float32)
    class_count = lax.optimization_barrier(jnp.sum(slot_hot.astype(jnp.float32), axis=0))
    anchor_category_ids = owned_sums[row_slot]
    same_category_tally = jnp.maximum(class_count[row_slot] - 1.0, 1.0)
    unit_vectors_single_precise = unit_vectors_brain16.astype(jnp.float32)
    feature_vector_derivative = anchor_target_share / sharpness_divisor - 2.0 * (anchor_category_ids - unit_vectors_single_precise) / (sharpness_divisor * same_category_tally[:, None])
    radial = lax.optimization_barrier(jnp.sum(unit * feature_vector_derivative, axis=1, keepdims=True))
    projected_grad = (inv_norm * (feature_vector_derivative - unit * radial)).astype(jnp.bfloat16)
    weight_grad = lax.dot_general(features, projected_grad, (((0,), (0,)), ((), ())), preferred_element_type=jnp.float32)
    return (projected_grad, weight_grad, owned_sums)
```

```python
import jax
import jax.numpy as jnp
from jax import lax
from jax.experimental import pallas as pl
from jax.experimental.pallas import tpu as pltpu
from jax.sharding import PartitionSpec as P

MESH = pl.DeviceIdType.MESH
SIDE = 4
ROWS = 128
FEATURES = 1024
WIDTH = 512
CLASSES = 512
ROW_BLOCKS = 8
COL_BLOCKS = 16
LINE = SIDE * ROWS
N_COPIES = 80
INV_SHARPNESS = 10.0
LOG2_SCALE = 14.426950408889634
F32 = jnp.float32
BF16 = jnp.bfloat16


def dot(a, b):
    return jnp.dot(a, b, preferred_element_type=F32)


def dot_nt(a, b):
    return lax.dot_general(a, b, (((1,), (1,)), ((), ())), preferred_element_type=F32)


class Copies:
    def __init__(self, send_sems, recv_sems, any_device):
        self.send_sems, self.recv_sems, self.any_device = send_sems, recv_sems, any_device
        self.used = 0
        self.started = []

    def _copy(self, src, dst, k, device):
        return pltpu.make_async_remote_copy(
            src_ref=src,
            dst_ref=dst,
            send_sem=self.send_sems.at[k],
            recv_sem=self.recv_sems.at[k],
            device_id=device,
            device_id_type=MESH,
        )

    def send(self, src, dst, device):
        k = self.used
        self.used += 1
        copy = self._copy(src, dst, k, device)
        copy.start()
        self.started.append(copy)
        return k

    def arrived(self, dst, k):
        self._copy(dst, dst, k, self.any_device).wait_recv()

    def finish(self):
        for copy in self.started:
            copy.wait_send()


def kernel(
    feat,
    wgt,
    lab,
    slots,
    pg_out,
    wg_out,
    own_out,
    ucol,
    urow,
    unit_s,
    inv_s,
    feat_t,
    e,
    lcol,
    lrow,
    rlab,
    racc,
    rcnt,
    rinv,
    pinv,
    cinv,
    csum,
    cz1,
    cz2,
    trow,
    tz1,
    tz2,
    mu,
    osib,
    orecv,
    zsend,
    zrecv,
    g_sib,
    g_sib_recv,
    g_own,
    g_zsend,
    g_zrecv,
    g_xsend,
    g_xrecv,
    g_ysend,
    g_yrecv,
    s_part,
    s_recv,
    s_zrecv,
    send_sems,
    recv_sems,
):
    dp = lax.axis_index("dp")
    y = lax.axis_index("grp")
    c = lax.rem(dp, 2)
    x = lax.rem(lax.div(dp, 2), SIDE)
    z = lax.div(dp, 2 * SIDE)
    other = 1 - c
    p = other * x + c * y
    q = other * y + c * x

    def ring(v, o):
        return lax.rem(v + o, SIDE)

    def at(z_, x_, c_, y_):
        return ((z_ * SIDE + x_) * 2 + c_, y_)

    def at_pq(p_, q_):
        return at(z, other * p_ + c * q_, c, other * q_ + c * p_)

    sib = at(z, x, other, y)
    p_dev = [None] + [at_pq(ring(p, o), q) for o in (1, 2, 3)]
    q_dev = [None] + [at_pq(p, ring(q, o)) for o in (1, 2, 3)]
    z_dev = [None] + [at(ring(z, o), x, c, y) for o in (1, 2, 3)]
    x_dev = [None] + [at(z, ring(x, o), c, y) for o in (1, 2, 3)]
    y_dev = [None] + [at(z, x, c, ring(y, o)) for o in (1, 2, 3)]
    peers = [sib] + z_dev[1:] + x_dev[1:] + y_dev[1:]

    barrier = pltpu.get_barrier_semaphore()
    for peer in peers:
        pl.semaphore_signal(barrier, inc=1, device_id=peer, device_id_type=MESH)

    cp = Copies(send_sems, recv_sems, sib)
    my_col = q * SIDE + p
    my_row = c * SIDE + z

    projected = dot(feat[...], wgt[...])
    inv_norm = lax.rsqrt(jnp.sum(projected * projected, axis=1, keepdims=True) + 1e-06)
    unit = projected * inv_norm
    unit_s[...] = unit
    inv_s[...] = inv_norm
    u16 = unit.astype(BF16)
    ucol[my_col] = u16
    urow[my_row] = u16
    my_lab = lab[...].astype(F32)
    lcol[my_col] = my_lab
    lrow[my_row] = my_lab

    pl.semaphore_wait(barrier, len(peers))

    lab_p = [cp.send(lcol.at[my_col], lcol.at[my_col], p_dev[o]) for o in (1, 2, 3)]
    lab_z = [cp.send(lrow.at[my_row], lrow.at[my_row], z_dev[o]) for o in (1, 2, 3)]

    def whole(ref, slot):
        return ref.at[slot]

    def low(ref, slot):
        return ref.at[slot, pl.ds(0, ROWS // 2)]

    def high(ref, slot):
        return ref.at[slot, pl.ds(ROWS // 2, ROWS // 2)]

    def ring_send(ref, slot, devs):
        return [cp.send(whole(ref, slot), whole(ref, slot), devs[o]) for o in (1, 3)]

    def ring_pass_up(ref, ids, slot, devs):
        cp.arrived(whole(ref, slot), ids[0])
        return cp.send(low(ref, slot), low(ref, slot), devs[1])

    def ring_pass_down(ref, ids, slot, devs):
        cp.arrived(whole(ref, slot), ids[1])
        return cp.send(high(ref, slot), high(ref, slot), devs[3])

    def ring_far(ref, up, down, slot):
        cp.arrived(low(ref, slot), up)
        cp.arrived(high(ref, slot), down)

    def col(o_p, o_q):
        return ring(q, o_q) * SIDE + ring(p, o_p)

    def row(o_z):
        return c * SIDE + ring(z, o_z)

    def row_sib(o_z):
        return other * SIDE + ring(z, o_z)

    p_ids = ring_send(ucol, my_col, p_dev)
    z_ids = ring_send(urow, my_row, z_dev)
    q_ids = {0: ring_send(ucol, my_col, q_dev)}
    sib_ids = {0: cp.send(urow.at[my_row], urow.at[my_row], sib)}

    for o in (1, 2, 3):
        cp.arrived(lcol.at[col(SIDE - o, 0)], lab_p[o - 1])
        cp.arrived(lrow.at[row(SIDE - o)], lab_z[o - 1])
    my_line = lcol.at[pl.ds(q * SIDE, SIDE)]
    lab_q = [cp.send(my_line, my_line, q_dev[o]) for o in (1, 2, 3)]
    my_set = lrow.at[pl.ds(c * SIDE, SIDE)]
    lab_s = cp.send(my_set, my_set, sib)

    p_up = ring_pass_up(ucol, p_ids, col(3, 0), p_dev)
    q_ids[3] = ring_send(ucol, col(3, 0), q_dev)
    p_down = ring_pass_down(ucol, p_ids, col(1, 0), p_dev)
    q_ids[1] = ring_send(ucol, col(1, 0), q_dev)
    z_up = ring_pass_up(urow, z_ids, row(3), z_dev)
    sib_ids[3] = cp.send(urow.at[row(3)], urow.at[row(3)], sib)
    z_down = ring_pass_down(urow, z_ids, row(1), z_dev)
    sib_ids[1] = cp.send(urow.at[row(1)], urow.at[row(1)], sib)

    for o in (1, 2, 3):
        line = lcol.at[pl.ds(ring(q, SIDE - o) * SIDE, SIDE)]
        cp.arrived(line, lab_q[o - 1])
    cp.arrived(lrow.at[pl.ds(other * SIDE, SIDE)], lab_s)

    ring_far(ucol, p_up, p_down, col(2, 0))
    q_ids[2] = ring_send(ucol, col(2, 0), q_dev)
    ring_far(urow, z_up, z_down, row(2))
    sib_ids[2] = cp.send(urow.at[row(2)], urow.at[row(2)], sib)

    q_up, q_down = {}, {}

    def q_pass(o_p):
        q_up[o_p] = ring_pass_up(ucol, q_ids[o_p], col(o_p, 3), q_dev)
        q_down[o_p] = ring_pass_down(ucol, q_ids[o_p], col(o_p, 1), q_dev)

    q_pass(0)

    lane = lax.broadcasted_iota(jnp.int32, (ROWS, ROWS), 1)

    def turned(block):
        pad = jnp.zeros((ROWS - block.shape[0], ROWS), F32)
        return jnp.transpose(jnp.concatenate([block, pad], axis=0))

    lab_t = turned(jnp.concatenate([lrow[k] for k in range(ROW_BLOCKS)], axis=0))
    for k in range(ROW_BLOCKS):
        rlab[k * ROWS : (k + 1) * ROWS, :] = lab_t[:, k : k + 1]

    def count_block(k, carry):
        rows = pl.ds(pl.multiple_of(k * ROWS, ROWS), ROWS)
        mine = rlab[rows, :]
        total = jnp.zeros((ROWS, ROWS), F32)
        for j in range(COL_BLOCKS):
            total = total + jnp.where(mine == lcol[j], 1.0, 0.0)
        rcnt[rows, :] = jnp.sum(total, axis=1, keepdims=True)
        racc[rows, :] = jnp.zeros((ROWS, ROWS), F32)
        return carry

    lax.fori_loop(0, ROW_BLOCKS, count_block, 0)

    q_pass(3)
    q_pass(1)

    for o in (0, 3, 1, 2):
        cp.arrived(urow.at[row_sib(o)], sib_ids[o])

    TILE = 256

    def line_tiles(q_, first, last, own_line, sums):
        keys = ucol[pl.ds(q_ * SIDE, SIDE)].reshape(LINE, WIDTH)
        row_base = my_row * ROWS
        col_base = p * ROWS

        def tile(r, sums):
            rows = pl.ds(pl.multiple_of(r * TILE, TILE), TILE)
            queries = urow[pl.ds(r * 2, 2)].reshape(TILE, WIDTH)
            value = jnp.exp2(dot_nt(queries, keys) * LOG2_SCALE)
            if own_line:
                i = lax.broadcasted_iota(jnp.int32, (TILE, LINE), 0) + (r * TILE - row_base)
                j = lax.broadcasted_iota(jnp.int32, (TILE, LINE), 1) - col_base
                value = jnp.where((i == j) & (j >= 0) & (j < ROWS), 0.0, value)
            e[q_, rows, :] = value
            racc[rows, :] += (
                value[:, 0:ROWS]
                + value[:, ROWS : 2 * ROWS]
                + value[:, 2 * ROWS : 3 * ROWS]
                + value[:, 3 * ROWS : 4 * ROWS]
            )
            return sums + jnp.sum(value.reshape(TILE // 8, 8, LINE), axis=0)

        return lax.fori_loop(first, last, tile, sums)

    no_sums = jnp.zeros((8, LINE), F32)

    def put_sums(q_, sums):
        total = jnp.sum(sums, axis=0, keepdims=True)
        for k in range(SIDE):
            csum[q_ * SIDE + k] = total[:, k * ROWS : (k + 1) * ROWS]

    sums = line_tiles(q, 0, 2, True, no_sums)
    q_pass(2)
    put_sums(q, line_tiles(q, 2, 4, True, sums))
    for o in (3, 1):
        put_sums(ring(q, o), line_tiles(ring(q, o), 0, 4, False, no_sums))
    feat_t[...] = jnp.transpose(feat[...]).reshape(COL_BLOCKS, 2, 32, ROWS)
    for o_p in (0, 3, 1, 2):
        ring_far(ucol, q_up[o_p], q_down[o_p], col(o_p, 2))
    put_sums(ring(q, 2), line_tiles(ring(q, 2), 0, 4, False, no_sums))

    table = jnp.zeros((ROWS, ROWS), F32)
    for k in range(ROW_BLOCKS):
        rows = slice(k * ROWS, (k + 1) * ROWS)
        table = jnp.where(lane == k, jnp.sum(racc[rows, :], axis=1, keepdims=True), table)
        table = jnp.where(lane == ROW_BLOCKS + k, rcnt[rows, :], table)
    trow[0] = jnp.transpose(table)[0 : 2 * ROW_BLOCKS, :]
    t_ids = [cp.send(trow.at[0], tz1.at[o - 1], z_dev[o]) for o in (1, 2, 3)]
    c_ids = [cp.send(csum, cz1.at[o - 1], p_dev[o]) for o in (1, 2, 3)]

    lab_lanes = jnp.concatenate([lcol[j] for j in range(COL_BLOCKS)], axis=1)

    def all_keys():
        return ucol[...].reshape(COL_BLOCKS * ROWS, WIDTH)

    def class_tile(r, carry):
        rows = pl.ds(pl.multiple_of(r * TILE, TILE), TILE)
        same = jnp.where(rlab[rows, :] == lab_lanes, 1.0, 0.0).astype(BF16)
        mu[rows, :] = dot(same, all_keys())
        return carry

    lax.fori_loop(0, 2, class_tile, 0)

    for o in (1, 2, 3):
        cp.arrived(tz1.at[o - 1], t_ids[o - 1])
        cp.arrived(cz1.at[o - 1], c_ids[o - 1])
    trow[1] = trow[0] + tz1[0] + tz1[1] + tz1[2]
    cz2[3] = csum[...] + cz1[0] + cz1[1] + cz1[2]
    t_id2 = cp.send(trow.at[1], tz2, sib)
    c_ids2 = [cp.send(cz2.at[3], cz2.at[o - 1], q_dev[o]) for o in (1, 2, 3)]

    lax.fori_loop(2, 4, class_tile, 0)

    rho = lax.broadcasted_iota(jnp.int32, (8 * ROW_BLOCKS, 1), 0)
    block, k_slot = rho // 8, rho % 8
    owner = (((block % SIDE) * SIDE + x) * 2 + block // SIDE) * SIDE + y
    wanted = jnp.where(k_slot < 4, owner * 4 + k_slot, -1)
    class_of = jnp.zeros((8 * ROW_BLOCKS, ROWS), F32)
    lane_row = lax.broadcasted_iota(jnp.int32, (8 * ROW_BLOCKS, ROWS), 1)
    for j in range(CLASSES // ROWS):
        hit = slots[j : j + 1, :] == wanted
        class_of = class_of + jnp.where(hit, (lane_row + (j * ROWS + 1)).astype(F32), 0.0)
    class_of = jnp.sum(class_of, axis=1, keepdims=True) - 1.0
    member = jnp.where(class_of == lab_lanes, 1.0, 0.0).astype(BF16)
    s_part[...] = dot(member, all_keys()).reshape(2, SIDE, 8, WIDTH)
    s_id = cp.send(s_part.at[other], s_recv, sib)

    cp.arrived(tz2, t_id2)
    totals = trow[1] + tz2[...]
    first = lax.broadcasted_iota(jnp.int32, (2 * ROW_BLOCKS, ROWS), 0) < ROW_BLOCKS
    scales = turned(1.0 / jnp.where(first, totals, jnp.maximum(totals - 1.0, 1.0)))
    for k in range(ROW_BLOCKS):
        rows = slice(k * ROWS, (k + 1) * ROWS)
        rinv[rows, :] = scales[:, k : k + 1]
        pinv[rows, :] = 2.0 * scales[:, ROW_BLOCKS + k : ROW_BLOCKS + k + 1]
    for o in (1, 2, 3):
        cp.arrived(cz2.at[o - 1], c_ids2[o - 1])
    cinv[...] = 1.0 / (cz2[0] + cz2[1] + cz2[2] + cz2[3])
    cinv_lines = [
        jnp.concatenate([cinv[l * SIDE + k] for k in range(SIDE)], axis=1) for l in range(SIDE)
    ]

    def gradient(rows):
        scale = rinv[rows, :]
        weights = jnp.concatenate(
            [(e[l, rows, :] * (scale + cinv_lines[l])).astype(BF16) for l in range(SIDE)], axis=1
        )
        return dot(weights, all_keys()) - pinv[rows, :] * mu[rows, :]

    o_ids = []
    for h in range(2):
        rows = pl.ds(pl.multiple_of(other * LINE + h * TILE, TILE), TILE)
        half = pl.ds(h * TILE, TILE)
        osib[half, :] = gradient(rows)
        o_ids.append(cp.send(osib.at[half], orecv.at[half], sib))

    cp.arrived(s_recv, s_id)
    s_recv[...] = s_recv[...] + s_part[c]
    s_ids = [cp.send(s_recv.at[ring(z, o)], s_zrecv.at[o - 1], z_dev[o]) for o in (1, 2, 3)]

    o_zids = {}
    for n, o in enumerate((2, 1, 3, 0)):
        z_ = ring(z, o)
        rows = pl.ds(pl.multiple_of((c * SIDE + z_) * ROWS, ROWS), ROWS)
        part = gradient(rows)
        if n == 0:
            for h in range(2):
                half = pl.ds(h * TILE, TILE)
                cp.arrived(orecv.at[half], o_ids[h])
        there = pl.ds(pl.multiple_of(z_ * ROWS, ROWS), ROWS)
        part = part + orecv[there, :]
        if o:
            zsend[o - 1] = part.astype(BF16)
            o_zids[o] = cp.send(zsend.at[o - 1], zrecv.at[o - 1], z_dev[o])
    my_rows = pl.ds(pl.multiple_of(my_row * ROWS, ROWS), ROWS)
    part = part + pinv[my_rows, :] * urow[my_row].astype(F32)
    for o in (1, 2, 3):
        cp.arrived(s_zrecv.at[o - 1], s_ids[o - 1])
    own_out[...] = (s_recv[z] + s_zrecv[0] + s_zrecv[1] + s_zrecv[2])[0:4, :]
    for o in (1, 3, 2):
        cp.arrived(zrecv.at[o - 1], o_zids[o])
        part = part + zrecv[o - 1].astype(F32)
    part = part * INV_SHARPNESS
    unit = unit_s[...]
    radial = jnp.sum(unit * part, axis=1, keepdims=True)
    pg = (inv_s[...] * (part - unit * radial)).astype(BF16)
    pg_out[...] = pg

    g_sib[...] = dot(feat_t[:, other].reshape(LINE, ROWS), pg).reshape(g_sib.shape)
    g_id = cp.send(g_sib, g_sib_recv, sib)
    mine = dot(feat_t[:, c].reshape(LINE, ROWS), pg).reshape(COL_BLOCKS, 32, WIDTH)
    g_own[...] = mine
    cp.arrived(g_sib_recv, g_id)

    def z_part(z_):
        runs = pl.ds(z_ * SIDE, SIDE)
        return g_own[runs] + g_sib_recv[runs]

    ids = {}
    for o in (2, 1, 3):
        g_zsend[o - 1] = z_part(ring(z, o)).astype(BF16)
        ids[o] = cp.send(g_zsend.at[o - 1], g_zrecv.at[o - 1], z_dev[o])
    z_total = z_part(z)
    for o in (1, 3, 2):
        cp.arrived(g_zrecv.at[o - 1], ids[o])
    g_own[pl.ds(0, SIDE)] = (
        z_total
        + g_zrecv[0].astype(F32)
        + g_zrecv[1].astype(F32)
        + g_zrecv[2].astype(F32)
    )
    for o in (2, 1, 3):
        g_xsend[o - 1] = g_own[ring(x, o)]
        ids[o] = cp.send(g_xsend.at[o - 1], g_xrecv.at[o - 1], x_dev[o])
    part = g_own[x]
    for o in (1, 3, 2):
        cp.arrived(g_xrecv.at[o - 1], ids[o])
        part = part + g_xrecv[o - 1]
    g_ysend[...] = part.reshape(SIDE, 8, WIDTH)
    for o in (2, 1, 3):
        ids[o] = cp.send(g_ysend.at[ring(y, o)], g_yrecv.at[o - 1], y_dev[o])
    part = g_ysend[y]
    for o in (1, 3, 2):
        cp.arrived(g_yrecv.at[o - 1], ids[o])
        part = part + g_yrecv[o - 1]
    wg_out[...] = part

    cp.finish()


def body(features, proj_weight, labels, owner_slot):
    vmem = pl.BlockSpec(memory_space=pltpu.VMEM)
    rows_all = ROW_BLOCKS * ROWS
    scratch = [
        pltpu.VMEM((COL_BLOCKS, ROWS, WIDTH), BF16),
        pltpu.VMEM((ROW_BLOCKS, ROWS, WIDTH), BF16),
        pltpu.VMEM((ROWS, WIDTH), F32),
        pltpu.VMEM((ROWS, 1), F32),
        pltpu.VMEM((COL_BLOCKS, 2, 32, ROWS), BF16),
        pltpu.VMEM((SIDE, rows_all, LINE), F32),
        pltpu.VMEM((COL_BLOCKS, 1, ROWS), F32),
        pltpu.VMEM((ROW_BLOCKS, 1, ROWS), F32),
        pltpu.VMEM((rows_all, 1), F32),
        pltpu.VMEM((rows_all, ROWS), F32),
        pltpu.VMEM((rows_all, 1), F32),
        pltpu.VMEM((rows_all, 1), F32),
        pltpu.VMEM((rows_all, 1), F32),
        pltpu.VMEM((COL_BLOCKS, 1, ROWS), F32),
        pltpu.VMEM((COL_BLOCKS, 1, ROWS), F32),
        pltpu.VMEM((3, COL_BLOCKS, 1, ROWS), F32),
        pltpu.VMEM((4, COL_BLOCKS, 1, ROWS), F32),
        pltpu.VMEM((2, 2 * ROW_BLOCKS, ROWS), F32),
        pltpu.VMEM((3, 2 * ROW_BLOCKS, ROWS), F32),
        pltpu.VMEM((2 * ROW_BLOCKS, ROWS), F32),
        pltpu.VMEM((rows_all, WIDTH), F32),
        pltpu.VMEM((LINE, WIDTH), F32),
        pltpu.VMEM((LINE, WIDTH), F32),
        pltpu.VMEM((3, ROWS, WIDTH), BF16),
        pltpu.VMEM((3, ROWS, WIDTH), BF16),
        pltpu.VMEM((COL_BLOCKS, 32, WIDTH), F32),
        pltpu.VMEM((COL_BLOCKS, 32, WIDTH), F32),
        pltpu.VMEM((COL_BLOCKS, 32, WIDTH), F32),
        pltpu.VMEM((3, SIDE, 32, WIDTH), BF16),
        pltpu.VMEM((3, SIDE, 32, WIDTH), BF16),
        pltpu.VMEM((3, 32, WIDTH), F32),
        pltpu.VMEM((3, 32, WIDTH), F32),
        pltpu.VMEM((SIDE, 8, WIDTH), F32),
        pltpu.VMEM((3, 8, WIDTH), F32),
        pltpu.VMEM((2, SIDE, 8, WIDTH), F32),
        pltpu.VMEM((SIDE, 8, WIDTH), F32),
        pltpu.VMEM((3, 8, WIDTH), F32),
        pltpu.SemaphoreType.DMA((N_COPIES,)),
        pltpu.SemaphoreType.DMA((N_COPIES,)),
    ]
    return pl.pallas_call(
        kernel,
        out_shape=(
            jax.ShapeDtypeStruct((ROWS, WIDTH), BF16),
            jax.ShapeDtypeStruct((8, WIDTH), F32),
            jax.ShapeDtypeStruct((4, WIDTH), F32),
        ),
        in_specs=[vmem] * 4,
        out_specs=(vmem,) * 3,
        scratch_shapes=scratch,
        compiler_params=pltpu.CompilerParams(
            collective_id=0, has_side_effects=True, vmem_limit_bytes=56 * 1024 * 1024
        ),
        name="contrastive",
    )(features, proj_weight, labels.reshape(1, ROWS), owner_slot.reshape(CLASSES // ROWS, ROWS))


def solution(mesh):
    in_specs = (P(("dp", "grp"), None), P(), P(("dp", "grp")), P())
    out_specs = (P(("dp", "grp"), None), P(("dp", "grp"), None), P(("dp", "grp"), None))
    return jax.shard_map(body, mesh=mesh, in_specs=in_specs, out_specs=out_specs, check_vma=False)
```

```python
import jax
import jax.numpy as jnp
from jax import lax
from jax.experimental import pallas as pl
from jax.experimental.pallas import tpu as pltpu
from jax.sharding import PartitionSpec as P

MESH = pl.DeviceIdType.MESH
SIDE = 4
ROWS = 128
FEATURES = 1024
WIDTH = 512
CLASSES = 512
ROW_BLOCKS = 8
COL_BLOCKS = 16
LINE = SIDE * ROWS
N_COPIES = 120
RING = (1, 3, 2)
PLANE = tuple(sorted(((a, b) for a in range(4) for b in range(4) if a or b), key=lambda o: -(min(o[0], 4 - o[0]) + min(o[1], 4 - o[1]))))
INV_SHARPNESS = 10.0
LOG2_SCALE = 14.426950408889634
F32 = jnp.float32
BF16 = jnp.bfloat16


def dot(a, b):
    return jnp.dot(a, b, preferred_element_type=F32)


def dot_nt(a, b):
    return lax.dot_general(a, b, (((1,), (1,)), ((), ())), preferred_element_type=F32)


class Copies:
    def __init__(self, send_sems, recv_sems, any_device):
        self.send_sems, self.recv_sems, self.any_device = send_sems, recv_sems, any_device
        self.used = 0
        self.started = []

    def _copy(self, src, dst, k, device):
        return pltpu.make_async_remote_copy(
            src_ref=src,
            dst_ref=dst,
            send_sem=self.send_sems.at[k],
            recv_sem=self.recv_sems.at[k],
            device_id=device,
            device_id_type=MESH,
        )

    def send(self, src, dst, device):
        k = self.used
        self.used += 1
        copy = self._copy(src, dst, k, device)
        copy.start()
        self.started.append(copy)
        return k

    def arrived(self, dst, k):
        self._copy(dst, dst, k, self.any_device).wait_recv()

    def finish(self, keep=0):
        done = len(self.started) - keep
        for copy in self.started[:done]:
            copy.wait_send()
        self.started = self.started[done:]


def kernel(
    feat_hbm,
    wgt_hbm,
    lab,
    slots,
    pg_out,
    wg_out,
    own_out,
    feat,
    wgt,
    ucol,
    urow,
    ulow,
    frow,
    feat_t,
    e,
    lcol,
    lrow,
    rlab,
    rnorm,
    racc,
    rcnt,
    rinv,
    pinv,
    csum,
    cz,
    trow,
    tz,
    mu,
    osib,
    orecv,
    obuf,
    dpart,
    g_sib,
    g_sib_recv,
    zsend,
    zrecv,
    g_own,
    g_send,
    g_recv,
    g_zsend,
    g_zrecv,
    s_part,
    s_recv,
    s_zrecv,
    send_sems,
    recv_sems,
    load_sems,
):
    dp = lax.axis_index("dp")
    y = lax.axis_index("grp")
    c = lax.rem(dp, 2)
    x = lax.rem(lax.div(dp, 2), SIDE)
    z = lax.div(dp, 2 * SIDE)
    other = 1 - c
    p = other * x + c * y
    q = other * y + c * x

    def ring(v, o):
        return lax.rem(v + o, SIDE)

    def at(z_, x_, c_, y_):
        return ((z_ * SIDE + x_) * 2 + c_, y_)

    def at_pq(p_, q_):
        return at(z, other * p_ + c * q_, c, other * q_ + c * p_)

    sib = at(z, x, other, y)
    p_dev = [None] + [at_pq(ring(p, o), q) for o in (1, 2, 3)]
    q_dev = [None] + [at_pq(p, ring(q, o)) for o in (1, 2, 3)]
    z_dev = [None] + [at(ring(z, o), x, c, y) for o in (1, 2, 3)]
    z_sib = [sib] + [at(ring(z, o), x, other, y) for o in (1, 2, 3)]
    plane = {(a, b): at(z, ring(x, a), c, ring(y, b)) for a, b in PLANE}
    peers = list(plane.values()) + z_dev[1:] + z_sib

    barrier = pltpu.get_barrier_semaphore()
    for peer in peers:
        pl.semaphore_signal(barrier, inc=1, device_id=peer, device_id_type=MESH)

    cp = Copies(send_sems, recv_sems, sib)
    my_col = q * SIDE + p
    my_row = c * SIDE + z

    loads = [
        pltpu.make_async_copy(feat_hbm, feat, load_sems.at[0]),
        pltpu.make_async_copy(wgt_hbm, wgt, load_sems.at[1]),
    ]
    for load in loads:
        load.start()
    for load in loads:
        load.wait()

    projected = dot(feat[...], wgt[...])
    inv_norm = lax.rsqrt(jnp.sum(projected * projected, axis=1, keepdims=True) + 1e-06)
    unit = projected * inv_norm
    u16 = unit.astype(BF16)
    ulow[my_row] = (unit - u16.astype(F32)).astype(BF16)
    ucol[my_col] = u16
    urow[my_row] = u16
    my_lab = lab[...].astype(F32)
    lcol[my_col] = my_lab
    inv_lanes = jnp.transpose(jnp.broadcast_to(inv_norm, (ROWS, ROWS)))[0:1, :]
    lrow[my_row] = jnp.concatenate([my_lab, inv_lanes], axis=0)

    pl.semaphore_wait(barrier, len(peers))

    lab_p = {o: cp.send(lcol.at[my_col], lcol.at[my_col], p_dev[o]) for o in RING}
    lab_z = {o: cp.send(lrow.at[my_row], lrow.at[my_row], z_dev[o]) for o in RING}

    def col(o_p, o_q):
        return ring(q, o_q) * SIDE + ring(p, o_p)

    def row(o_z):
        return c * SIDE + ring(z, o_z)

    def row_sib(o_z):
        return other * SIDE + ring(z, o_z)

    def spread(ref, slot, devs):
        return {o: cp.send(ref.at[slot], ref.at[slot], devs[o]) for o in RING}

    p_ids = spread(ucol, my_col, p_dev)
    z_ids = spread(urow, my_row, z_dev)
    q_ids = {0: spread(ucol, my_col, q_dev)}
    sib_ids = {0: cp.send(urow.at[my_row], urow.at[my_row], sib)}

    turn = jnp.transpose(feat[...].astype(F32)).reshape(SIDE, SIDE, 2, SIDE, 8, ROWS)
    for z_ in range(SIDE):
        for x_ in range(SIDE):
            for c_ in range(2):
                for y_ in range(SIDE):
                    feat_t[c_, x_, y_, z_] = turn[z_, x_, c_, y_]
    frow[my_row] = feat_t[...].reshape(FEATURES, ROWS).astype(BF16)

    for o in RING:
        cp.arrived(lcol.at[col(SIDE - o, 0)], lab_p[o])
        cp.arrived(lrow.at[row(SIDE - o)], lab_z[o])
    my_line = lcol.at[pl.ds(q * SIDE, SIDE)]
    lab_q = {o: cp.send(my_line, my_line, q_dev[o]) for o in RING}
    my_set = lrow.at[pl.ds(c * SIDE, SIDE)]
    lab_s = cp.send(my_set, my_set, sib)

    for o in RING:
        back = SIDE - o
        cp.arrived(ucol.at[col(back, 0)], p_ids[o])
        q_ids[back] = spread(ucol, col(back, 0), q_dev)
        cp.arrived(urow.at[row(back)], z_ids[o])
        sib_ids[back] = cp.send(urow.at[row(back)], urow.at[row(back)], sib)

    late_z = [(ref, spread(ref, my_row, z_dev)) for ref in (ulow, frow)]
    late_s = [(ref, {0: cp.send(ref.at[my_row], ref.at[my_row], sib)}) for ref in (ulow, frow)]

    for o in RING:
        line = lcol.at[pl.ds(ring(q, SIDE - o) * SIDE, SIDE)]
        cp.arrived(line, lab_q[o])
    cp.arrived(lrow.at[pl.ds(other * SIDE, SIDE)], lab_s)

    lane = lax.broadcasted_iota(jnp.int32, (ROWS, ROWS), 1)

    def turned(block):
        pad = jnp.zeros((ROWS - block.shape[0], ROWS), F32)
        return jnp.transpose(jnp.concatenate([block, pad], axis=0))

    lab_t = turned(jnp.concatenate([lrow[k] for k in range(ROW_BLOCKS)], axis=0))
    for k in range(ROW_BLOCKS):
        rlab[k * ROWS : (k + 1) * ROWS, :] = lab_t[:, 2 * k : 2 * k + 1]
        rnorm[k * ROWS : (k + 1) * ROWS, :] = lab_t[:, 2 * k + 1 : 2 * k + 2] * INV_SHARPNESS

    def count_block(k, carry):
        rows = pl.ds(pl.multiple_of(k * ROWS, ROWS), ROWS)
        mine = rlab[rows, :]
        total = jnp.zeros((ROWS, ROWS), F32)
        for j in range(COL_BLOCKS):
            total = total + jnp.where(mine == lcol[j], 1.0, 0.0)
        rcnt[rows, :] = jnp.sum(total, axis=1, keepdims=True)
        racc[rows, :] = jnp.zeros((ROWS, ROWS), F32)
        return carry

    lax.fori_loop(0, ROW_BLOCKS, count_block, 0)

    for o in (0, 3, 1, 2):
        cp.arrived(urow.at[row_sib(o)], sib_ids[o])

    TILE = 256

    def line_tiles(q_, first, last, own_line, sums):
        keys = ucol[pl.ds(q_ * SIDE, SIDE)].reshape(LINE, WIDTH)
        row_base = my_row * ROWS
        col_base = p * ROWS

        def tile(r, sums):
            rows = pl.ds(pl.multiple_of(r * TILE, TILE), TILE)
            queries = urow[pl.ds(r * 2, 2)].reshape(TILE, WIDTH)
            value = jnp.exp2(dot_nt(queries, keys) * LOG2_SCALE)
            if own_line:
                i = lax.broadcasted_iota(jnp.int32, (TILE, LINE), 0) + (r * TILE - row_base)
                j = lax.broadcasted_iota(jnp.int32, (TILE, LINE), 1) - col_base
                value = jnp.where((i == j) & (j >= 0) & (j < ROWS), 0.0, value)
            e[q_, rows, :] = value
            racc[rows, :] += (
                value[:, 0:ROWS]
                + value[:, ROWS : 2 * ROWS]
                + value[:, 2 * ROWS : 3 * ROWS]
                + value[:, 3 * ROWS : 4 * ROWS]
            )
            return sums + jnp.sum(value.reshape(TILE // 8, 8, LINE), axis=0)

        return lax.fori_loop(first, last, tile, sums)

    no_sums = jnp.zeros((8, LINE), F32)

    def put_sums(q_, sums):
        total = jnp.sum(sums, axis=0, keepdims=True)
        for k in range(SIDE):
            csum[pl.ds(q_ * SIDE + k, 1), :] = total[:, k * ROWS : (k + 1) * ROWS]

    put_sums(q, line_tiles(q, 0, 4, True, no_sums))
    for o in RING:
        for o_p in (0, 3, 1, 2):
            cp.arrived(ucol.at[col(o_p, SIDE - o)], q_ids[o_p][o])
        q_ = ring(q, SIDE - o)
        put_sums(q_, line_tiles(q_, 0, 4, False, no_sums))

    table = jnp.zeros((ROWS, ROWS), F32)
    for k in range(ROW_BLOCKS):
        rows = slice(k * ROWS, (k + 1) * ROWS)
        table = jnp.where(lane == k, jnp.sum(racc[rows, :], axis=1, keepdims=True), table)
        table = jnp.where(lane == ROW_BLOCKS + k, rcnt[rows, :], table)
    trow[...] = jnp.transpose(table)[0 : 2 * ROW_BLOCKS, :]
    t_ids = {}
    for o in RING:
        t_ids[o] = cp.send(trow, tz.at[o], z_dev[o])
        t_ids[4 + o] = cp.send(trow, tz.at[4 + o], z_sib[o])
    t_ids[4] = cp.send(trow, tz.at[4], sib)
    c_ids = {o: cp.send(csum, cz.at[o[0] * SIDE + o[1]], plane[o]) for o in PLANE}

    lab_lanes = jnp.concatenate([lcol[j] for j in range(COL_BLOCKS)], axis=1)

    def all_keys():
        return ucol[...].reshape(COL_BLOCKS * ROWS, WIDTH)

    def class_tile(r, carry):
        rows = pl.ds(pl.multiple_of(r * TILE, TILE), TILE)
        same = jnp.where(rlab[rows, :] == lab_lanes, 1.0, 0.0).astype(BF16)
        mu[rows, :] = dot(same, all_keys())
        return carry

    lax.fori_loop(0, 4, class_tile, 0)
    my_rows = pl.ds(pl.multiple_of(my_row * ROWS, ROWS), ROWS)
    mu[my_rows, :] = mu[my_rows, :] - urow[my_row].astype(F32)

    rho = lax.broadcasted_iota(jnp.int32, (8 * ROW_BLOCKS, 1), 0)
    block, k_slot = rho // 8, rho % 8
    owner = (((block % SIDE) * SIDE + x) * 2 + block // SIDE) * SIDE + y
    wanted = jnp.where(k_slot < 4, owner * 4 + k_slot, -1)
    class_of = jnp.zeros((8 * ROW_BLOCKS, ROWS), F32)
    lane_row = lax.broadcasted_iota(jnp.int32, (8 * ROW_BLOCKS, ROWS), 1)
    for j in range(CLASSES // ROWS):
        hit = slots[j : j + 1, :] == wanted
        class_of = class_of + jnp.where(hit, (lane_row + (j * ROWS + 1)).astype(F32), 0.0)
    class_of = jnp.sum(class_of, axis=1, keepdims=True) - 1.0
    member = jnp.where(class_of == lab_lanes, 1.0, 0.0).astype(BF16)
    s_part[...] = dot(member, all_keys()).reshape(2, SIDE, 8, WIDTH)
    s_id = cp.send(s_part.at[other], s_recv, sib)

    for (ref, z_sent), (_, s_sent) in zip(late_z, late_s):
        for o in RING:
            back = SIDE - o
            cp.arrived(ref.at[row(back)], z_sent[o])
            s_sent[back] = cp.send(ref.at[row(back)], ref.at[row(back)], sib)
    cp.finish()

    totals = trow[...]
    for o in t_ids:
        cp.arrived(tz.at[o], t_ids[o])
        totals = totals + tz[o]
    first = lax.broadcasted_iota(jnp.int32, (2 * ROW_BLOCKS, ROWS), 0) < ROW_BLOCKS
    scales = turned(1.0 / jnp.where(first, totals, jnp.maximum(totals - 1.0, 1.0)))
    for k in range(ROW_BLOCKS):
        rows = slice(k * ROWS, (k + 1) * ROWS)
        rinv[rows, :] = scales[:, k : k + 1]
        pinv[rows, :] = 2.0 * scales[:, ROW_BLOCKS + k : ROW_BLOCKS + k + 1]
    col_totals = csum[...]
    for o in PLANE:
        cp.arrived(cz.at[o[0] * SIDE + o[1]], c_ids[o])
        col_totals = col_totals + cz[o[0] * SIDE + o[1]]
    cinv = 1.0 / col_totals
    cinv_lines = [
        jnp.concatenate([cinv[l * SIDE + k : l * SIDE + k + 1, :] for k in range(SIDE)], axis=1)
        for l in range(SIDE)
    ]

    def gradient(rows):
        scale = rinv[rows, :]
        weights = jnp.concatenate(
            [(e[l, rows, :] * (scale + cinv_lines[l])).astype(BF16) for l in range(SIDE)], axis=1
        )
        return dot(weights, all_keys()) - pinv[rows, :] * mu[rows, :]

    def project(part, rows, block, count):
        high = urow[pl.ds(block, count)].astype(F32).reshape(part.shape)
        unit = high + ulow[pl.ds(block, count)].astype(F32).reshape(part.shape)
        radial = jnp.sum(unit * part, axis=1, keepdims=True)
        return (rnorm[rows, :] * (part - unit * radial)).astype(BF16)

    def late_wait(o):
        for ref, s_sent in late_s:
            cp.arrived(ref.at[row_sib(o)], s_sent[o])

    for o in range(SIDE):
        late_wait(o)

    o_ids = []
    for c_, keep in ((other, osib), (c, obuf)):
        for h in range(2):
            first_row = c_ * LINE + h * TILE
            rows = pl.ds(pl.multiple_of(first_row, TILE), TILE)
            half = pl.ds(h * TILE, TILE)
            part = gradient(rows)
            keep[half, :] = part
            if keep is osib:
                o_ids.append(cp.send(osib.at[half], orecv.at[half], sib))
            dpart[rows, :] = project(part, rows, c_ * SIDE + 2 * h, 2)

    def feats(c_, h):
        runs = pl.ds(pl.multiple_of(c_ * LINE + h * TILE, TILE), TILE)
        return jnp.concatenate([frow[k, runs, :] for k in range(ROW_BLOCKS)], axis=1)

    gs_ids = []
    for h in range(2):
        half = pl.ds(h * TILE, TILE)
        g_sib[half] = dot(feats(other, h), dpart[...])
        gs_ids.append(cp.send(g_sib.at[half], g_sib_recv.at[half], sib))
    for h in range(2):
        g_own[pl.ds(2 * h, 2)] = dot(feats(c, h), dpart[...]).reshape(2, SIDE, 4 * 8, WIDTH)

    cp.arrived(s_recv, s_id)
    s_recv[...] = s_recv[...] + s_part[c]
    s_ids = [cp.send(s_recv.at[ring(z, o)], s_zrecv.at[o - 1], z_dev[o]) for o in (1, 2, 3)]

    o_zids = {}
    for h in range(2):
        cp.arrived(orecv.at[pl.ds(h * TILE, TILE)], o_ids[h])

    def rows_of(z_):
        there = pl.ds(pl.multiple_of(z_ * ROWS, ROWS), ROWS)
        return obuf[there, :] + orecv[there, :]

    for o in (2, 1, 3):
        zsend[o - 1] = rows_of(ring(z, o)).astype(BF16)
        o_zids[o] = cp.send(zsend.at[o - 1], zrecv.at[o - 1], z_dev[o])

    for h in range(2):
        half = pl.ds(h * TILE, TILE)
        cp.arrived(g_sib_recv.at[half], gs_ids[h])
        g_own[pl.ds(2 * h, 2)] = g_own[pl.ds(2 * h, 2)] + g_sib_recv[half].reshape(
            2, SIDE, 4 * 8, WIDTH
        )
    g_ids = {}
    for o in PLANE:
        k = o[0] * SIDE + o[1]
        g_send[k] = g_own[ring(x, o[0]), ring(y, o[1])].astype(BF16)
        g_ids[o] = cp.send(g_send.at[k], g_recv.at[k], plane[o])

    for o in (1, 2, 3):
        cp.arrived(s_zrecv.at[o - 1], s_ids[o - 1])
    own_out[...] = (s_recv[z] + s_zrecv[0] + s_zrecv[1] + s_zrecv[2])[0:4, :]
    part = rows_of(z)
    for o in (1, 3, 2):
        cp.arrived(zrecv.at[o - 1], o_zids[o])
        part = part + zrecv[o - 1].astype(F32)
    pg_out[...] = project(part, my_rows, my_row, 1)

    part = g_own[x, y]
    for o in PLANE[::-1]:
        k = o[0] * SIDE + o[1]
        cp.arrived(g_recv.at[k], g_ids[o])
        part = part + g_recv[k].astype(F32)
    g_zsend[...] = part.reshape(SIDE, 8, WIDTH)
    ids = {o: cp.send(g_zsend.at[ring(z, o)], g_zrecv.at[o - 1], z_dev[o]) for o in (2, 1, 3)}
    cp.finish(3)
    part = g_zsend[z]
    for o in (1, 3, 2):
        cp.arrived(g_zrecv.at[o - 1], ids[o])
        part = part + g_zrecv[o - 1]
    wg_out[...] = part

    cp.finish()


def body(features, proj_weight, labels, owner_slot):
    vmem = pl.BlockSpec(memory_space=pltpu.VMEM)
    rows_all = ROW_BLOCKS * ROWS
    scratch = [
        pltpu.VMEM((ROWS, FEATURES), BF16),
        pltpu.VMEM((FEATURES, WIDTH), BF16),
        pltpu.VMEM((COL_BLOCKS, ROWS, WIDTH), BF16),
        pltpu.VMEM((ROW_BLOCKS, ROWS, WIDTH), BF16),
        pltpu.VMEM((ROW_BLOCKS, ROWS, WIDTH), BF16),
        pltpu.VMEM((ROW_BLOCKS, FEATURES, ROWS), BF16),
        pltpu.VMEM((2, SIDE, SIDE, SIDE, 8, ROWS), F32),
        pltpu.VMEM((SIDE, rows_all, LINE), F32),
        pltpu.VMEM((COL_BLOCKS, 1, ROWS), F32),
        pltpu.VMEM((ROW_BLOCKS, 2, ROWS), F32),
        pltpu.VMEM((rows_all, 1), F32),
        pltpu.VMEM((rows_all, 1), F32),
        pltpu.VMEM((rows_all, ROWS), F32),
        pltpu.VMEM((rows_all, 1), F32),
        pltpu.VMEM((rows_all, 1), F32),
        pltpu.VMEM((rows_all, 1), F32),
        pltpu.VMEM((COL_BLOCKS, ROWS), F32),
        pltpu.VMEM((16, COL_BLOCKS, ROWS), F32),
        pltpu.VMEM((2 * ROW_BLOCKS, ROWS), F32),
        pltpu.VMEM((8, 2 * ROW_BLOCKS, ROWS), F32),
        pltpu.VMEM((rows_all, WIDTH), F32),
        pltpu.VMEM((LINE, WIDTH), F32),
        pltpu.VMEM((LINE, WIDTH), F32),
        pltpu.VMEM((LINE, WIDTH), F32),
        pltpu.VMEM((rows_all, WIDTH), BF16),
        pltpu.VMEM((LINE, WIDTH), F32),
        pltpu.VMEM((LINE, WIDTH), F32),
        pltpu.VMEM((3, ROWS, WIDTH), BF16),
        pltpu.VMEM((3, ROWS, WIDTH), BF16),
        pltpu.VMEM((SIDE, SIDE, 4 * 8, WIDTH), F32),
        pltpu.VMEM((16, 4 * 8, WIDTH), BF16),
        pltpu.VMEM((16, 4 * 8, WIDTH), BF16),
        pltpu.VMEM((SIDE, 8, WIDTH), F32),
        pltpu.VMEM((3, 8, WIDTH), F32),
        pltpu.VMEM((2, SIDE, 8, WIDTH), F32),
        pltpu.VMEM((SIDE, 8, WIDTH), F32),
        pltpu.VMEM((3, 8, WIDTH), F32),
        pltpu.SemaphoreType.DMA((N_COPIES,)),
        pltpu.SemaphoreType.DMA((N_COPIES,)),
        pltpu.SemaphoreType.DMA((2,)),
    ]
    return pl.pallas_call(
        kernel,
        out_shape=(
            jax.ShapeDtypeStruct((ROWS, WIDTH), BF16),
            jax.ShapeDtypeStruct((8, WIDTH), F32),
            jax.ShapeDtypeStruct((4, WIDTH), F32),
        ),
        in_specs=[pl.BlockSpec(memory_space=pl.ANY)] * 2 + [vmem] * 2,
        out_specs=(vmem,) * 3,
        scratch_shapes=scratch,
        compiler_params=pltpu.CompilerParams(
            collective_id=0, has_side_effects=True, vmem_limit_bytes=56 * 1024 * 1024
        ),
        name="contrastive",
    )(features, proj_weight, labels.reshape(1, ROWS), owner_slot.reshape(CLASSES // ROWS, ROWS))


def solution(mesh):
    in_specs = (P(("dp", "grp"), None), P(), P(("dp", "grp")), P())
    out_specs = (P(("dp", "grp"), None), P(("dp", "grp"), None), P(("dp", "grp"), None))
    return jax.shard_map(body, mesh=mesh, in_specs=in_specs, out_specs=out_specs, check_vma=False)
```

```python
import jax
import jax.numpy as jnp
from jax import lax
from jax.experimental import pallas as pl
from jax.experimental.pallas import tpu as pltpu
from jax.sharding import PartitionSpec as P

MESH = pl.DeviceIdType.MESH
SIDE = 4
ROWS = 128
FEATURES = 1024
WIDTH = 512
CLASSES = 512
ROW_BLOCKS = 8
COL_BLOCKS = 16
LINE = SIDE * ROWS
N_COPIES = 120
RING = (1, 3, 2)
PLANE = tuple(sorted(((a, b) for a in range(4) for b in range(4) if a or b), key=lambda o: -(min(o[0], 4 - o[0]) + min(o[1], 4 - o[1]))))
INV_SHARPNESS = 10.0
LOG2_SCALE = 14.426950408889634
F32 = jnp.float32
BF16 = jnp.bfloat16


def dot(a, b):
    return jnp.dot(a, b, preferred_element_type=F32)


def dot_nt(a, b):
    return lax.dot_general(a, b, (((1,), (1,)), ((), ())), preferred_element_type=F32)


class Copies:
    def __init__(self, send_sems, recv_sems, any_device):
        self.send_sems, self.recv_sems, self.any_device = send_sems, recv_sems, any_device
        self.used = 0
        self.started = []

    def _copy(self, src, dst, k, device):
        return pltpu.make_async_remote_copy(
            src_ref=src,
            dst_ref=dst,
            send_sem=self.send_sems.at[k],
            recv_sem=self.recv_sems.at[k],
            device_id=device,
            device_id_type=MESH,
        )

    def send(self, src, dst, device):
        k = self.used
        self.used += 1
        copy = self._copy(src, dst, k, device)
        copy.start()
        self.started.append(copy)
        return k

    def arrived(self, dst, k):
        self._copy(dst, dst, k, self.any_device).wait_recv()

    def finish(self, keep=0):
        done = len(self.started) - keep
        for copy in self.started[:done]:
            copy.wait_send()
        self.started = self.started[done:]


def kernel(
    feat_hbm,
    wgt_hbm,
    lab,
    slots,
    pg_out,
    wg_out,
    own_out,
    feat,
    wgt,
    ucol,
    urow,
    ulow,
    frow,
    feat_t,
    e,
    lcol,
    lrow,
    rlab,
    rnorm,
    racc,
    rcnt,
    rinv,
    pinv,
    csum,
    cz,
    trow,
    tz,
    mu,
    osib,
    orecv,
    obuf,
    dpart,
    g_sib,
    g_sib_recv,
    zsend,
    zrecv,
    g_own,
    g_send,
    g_recv,
    g_zsend,
    g_zrecv,
    s_part,
    s_recv,
    s_zrecv,
    send_sems,
    recv_sems,
    load_sems,
):
    dp = lax.axis_index("dp")
    y = lax.axis_index("grp")
    c = lax.rem(dp, 2)
    x = lax.rem(lax.div(dp, 2), SIDE)
    z = lax.div(dp, 2 * SIDE)
    other = 1 - c
    p = other * x + c * y
    q = other * y + c * x

    def ring(v, o):
        return lax.rem(v + o, SIDE)

    def at(z_, x_, c_, y_):
        return ((z_ * SIDE + x_) * 2 + c_, y_)

    def at_pq(p_, q_):
        return at(z, other * p_ + c * q_, c, other * q_ + c * p_)

    sib = at(z, x, other, y)
    p_dev = [None] + [at_pq(ring(p, o), q) for o in (1, 2, 3)]
    q_dev = [None] + [at_pq(p, ring(q, o)) for o in (1, 2, 3)]
    z_dev = [None] + [at(ring(z, o), x, c, y) for o in (1, 2, 3)]
    z_sib = [sib] + [at(ring(z, o), x, other, y) for o in (1, 2, 3)]
    plane = {(a, b): at(z, ring(x, a), c, ring(y, b)) for a, b in PLANE}
    peers = list(plane.values()) + z_dev[1:] + z_sib

    barrier = pltpu.get_barrier_semaphore()
    for peer in peers:
        pl.semaphore_signal(barrier, inc=1, device_id=peer, device_id_type=MESH)

    cp = Copies(send_sems, recv_sems, sib)
    my_col = q * SIDE + p
    my_row = c * SIDE + z

    loads = [
        pltpu.make_async_copy(feat_hbm, feat, load_sems.at[0]),
        pltpu.make_async_copy(wgt_hbm, wgt, load_sems.at[1]),
    ]
    for load in loads:
        load.start()
    for load in loads:
        load.wait()

    projected = dot(feat[...], wgt[...])
    inv_norm = lax.rsqrt(jnp.sum(projected * projected, axis=1, keepdims=True) + 1e-06)
    unit = projected * inv_norm
    u16 = unit.astype(BF16)
    ulow[my_row] = (unit - u16.astype(F32)).astype(BF16)
    ucol[my_col] = u16
    urow[my_row] = u16
    my_lab = lab[...].astype(F32)
    lcol[my_col] = my_lab
    inv_lanes = jnp.transpose(jnp.broadcast_to(inv_norm, (ROWS, ROWS)))[0:1, :]
    lrow[my_row] = jnp.concatenate([my_lab, inv_lanes], axis=0)

    pl.semaphore_wait(barrier, len(peers))

    lab_p = {o: cp.send(lcol.at[my_col], lcol.at[my_col], p_dev[o]) for o in RING}
    lab_z = {o: cp.send(lrow.at[my_row], lrow.at[my_row], z_dev[o]) for o in RING}

    def col(o_p, o_q):
        return ring(q, o_q) * SIDE + ring(p, o_p)

    def row(o_z):
        return c * SIDE + ring(z, o_z)

    def row_sib(o_z):
        return other * SIDE + ring(z, o_z)

    def spread(ref, slot, devs, offsets=RING):
        return {o: cp.send(ref.at[slot], ref.at[slot], devs[o]) for o in offsets}

    p_ids = spread(ucol, my_col, p_dev, (1, 3))
    first_sent, cp.started = cp.started[-2:], cp.started[:-2]
    z_ids = spread(urow, my_row, z_dev)
    sib_ids = {0: cp.send(urow.at[my_row], urow.at[my_row], sib)}
    for copy in first_sent:
        copy.wait_send()
    p_ids.update(spread(ucol, my_col, p_dev, (2,)))
    q_ids = {0: spread(ucol, my_col, q_dev, (1, 3))}
    late_z = [(ulow, spread(ulow, my_row, z_dev))]

    turn = jnp.transpose(feat[...].astype(F32)).reshape(SIDE, SIDE, 2, SIDE, 8, ROWS)
    for z_ in range(SIDE):
        for x_ in range(SIDE):
            for c_ in range(2):
                for y_ in range(SIDE):
                    feat_t[c_, x_, y_, z_] = turn[z_, x_, c_, y_]
    frow[my_row] = feat_t[...].reshape(FEATURES, ROWS).astype(BF16)
    late_z.append((frow, spread(frow, my_row, z_dev)))

    for o in RING:
        cp.arrived(lcol.at[col(SIDE - o, 0)], lab_p[o])
        cp.arrived(lrow.at[row(SIDE - o)], lab_z[o])
    my_line = lcol.at[pl.ds(q * SIDE, SIDE)]
    lab_q = {o: cp.send(my_line, my_line, q_dev[o]) for o in RING}
    my_set = lrow.at[pl.ds(c * SIDE, SIDE)]
    lab_s = cp.send(my_set, my_set, sib)

    for o in (1, 3):
        back = SIDE - o
        cp.arrived(ucol.at[col(back, 0)], p_ids[o])
        q_ids[back] = spread(ucol, col(back, 0), q_dev, (1, 3))
    q_ids[0].update(spread(ucol, my_col, q_dev, (2,)))
    for back in (3, 1):
        q_ids[back].update(spread(ucol, col(back, 0), q_dev, (2,)))
    cp.arrived(ucol.at[col(2, 0)], p_ids[2])
    q_ids[2] = spread(ucol, col(2, 0), q_dev)
    for o in RING:
        back = SIDE - o
        cp.arrived(urow.at[row(back)], z_ids[o])
        sib_ids[back] = cp.send(urow.at[row(back)], urow.at[row(back)], sib)

    late_s = [(ref, {0: cp.send(ref.at[my_row], ref.at[my_row], sib)}) for ref in (ulow, frow)]

    for o in RING:
        line = lcol.at[pl.ds(ring(q, SIDE - o) * SIDE, SIDE)]
        cp.arrived(line, lab_q[o])
    cp.arrived(lrow.at[pl.ds(other * SIDE, SIDE)], lab_s)

    lane = lax.broadcasted_iota(jnp.int32, (ROWS, ROWS), 1)

    def turned(block):
        pad = jnp.zeros((ROWS - block.shape[0], ROWS), F32)
        return jnp.transpose(jnp.concatenate([block, pad], axis=0))

    lab_t = turned(jnp.concatenate([lrow[k] for k in range(ROW_BLOCKS)], axis=0))
    for k in range(ROW_BLOCKS):
        rlab[k * ROWS : (k + 1) * ROWS, :] = lab_t[:, 2 * k : 2 * k + 1]
        rnorm[k * ROWS : (k + 1) * ROWS, :] = lab_t[:, 2 * k + 1 : 2 * k + 2] * INV_SHARPNESS

    def count_block(k, carry):
        rows = pl.ds(pl.multiple_of(k * ROWS, ROWS), ROWS)
        mine = rlab[rows, :]
        total = jnp.zeros((ROWS, ROWS), F32)
        for j in range(COL_BLOCKS):
            total = total + jnp.where(mine == lcol[j], 1.0, 0.0)
        rcnt[rows, :] = jnp.sum(total, axis=1, keepdims=True)
        racc[rows, :] = jnp.zeros((ROWS, ROWS), F32)
        return carry

    lax.fori_loop(0, ROW_BLOCKS, count_block, 0)

    for o in (0, 3, 1, 2):
        cp.arrived(urow.at[row_sib(o)], sib_ids[o])

    TILE = 256

    def line_tiles(q_, own_line):
        keys = ucol[pl.ds(q_ * SIDE, SIDE)].reshape(LINE, WIDTH)
        queries = urow[...].reshape(ROW_BLOCKS * ROWS, WIDTH)
        value = jnp.exp2(dot_nt(queries, keys) * LOG2_SCALE)
        if own_line:
            i = lax.broadcasted_iota(jnp.int32, value.shape, 0) - my_row * ROWS
            j = lax.broadcasted_iota(jnp.int32, value.shape, 1) - p * ROWS
            value = jnp.where((i == j) & (j >= 0) & (j < ROWS), 0.0, value)
        e[q_] = value
        racc[...] += (
            value[:, 0:ROWS]
            + value[:, ROWS : 2 * ROWS]
            + value[:, 2 * ROWS : 3 * ROWS]
            + value[:, 3 * ROWS : 4 * ROWS]
        )
        return jnp.sum(value.reshape(ROW_BLOCKS * ROWS // 8, 8, LINE), axis=0)

    def put_sums(q_, sums):
        total = jnp.sum(sums, axis=0, keepdims=True)
        for k in range(SIDE):
            csum[pl.ds(q_ * SIDE + k, 1), :] = total[:, k * ROWS : (k + 1) * ROWS]

    put_sums(q, line_tiles(q, True))
    for o in RING:
        for o_p in (0, 3, 1, 2):
            cp.arrived(ucol.at[col(o_p, SIDE - o)], q_ids[o_p][o])
        q_ = ring(q, SIDE - o)
        put_sums(q_, line_tiles(q_, False))

    table = jnp.zeros((ROWS, ROWS), F32)
    for k in range(ROW_BLOCKS):
        rows = slice(k * ROWS, (k + 1) * ROWS)
        table = jnp.where(lane == k, jnp.sum(racc[rows, :], axis=1, keepdims=True), table)
        table = jnp.where(lane == ROW_BLOCKS + k, rcnt[rows, :], table)
    trow[...] = jnp.transpose(table)[0 : 2 * ROW_BLOCKS, :]
    t_ids = {}
    for o in RING:
        t_ids[o] = cp.send(trow, tz.at[o], z_dev[o])
        t_ids[4 + o] = cp.send(trow, tz.at[4 + o], z_sib[o])
    t_ids[4] = cp.send(trow, tz.at[4], sib)
    c_ids = {o: cp.send(csum, cz.at[o[0] * SIDE + o[1]], plane[o]) for o in PLANE}

    lab_lanes = jnp.concatenate([lcol[j] for j in range(COL_BLOCKS)], axis=1)

    def all_keys():
        return ucol[...].reshape(COL_BLOCKS * ROWS, WIDTH)

    def class_tile(r, carry):
        rows = pl.ds(pl.multiple_of(r * TILE, TILE), TILE)
        same = jnp.where(rlab[rows, :] == lab_lanes, 1.0, 0.0).astype(BF16)
        mu[rows, :] = dot(same, all_keys())
        return carry

    lax.fori_loop(0, 4, class_tile, 0)
    my_rows = pl.ds(pl.multiple_of(my_row * ROWS, ROWS), ROWS)
    mu[my_rows, :] = mu[my_rows, :] - urow[my_row].astype(F32)

    rho = lax.broadcasted_iota(jnp.int32, (8 * ROW_BLOCKS, 1), 0)
    block, k_slot = rho // 8, rho % 8
    owner = (((block % SIDE) * SIDE + x) * 2 + block // SIDE) * SIDE + y
    wanted = jnp.where(k_slot < 4, owner * 4 + k_slot, -1)
    class_of = jnp.zeros((8 * ROW_BLOCKS, ROWS), F32)
    lane_row = lax.broadcasted_iota(jnp.int32, (8 * ROW_BLOCKS, ROWS), 1)
    for j in range(CLASSES // ROWS):
        hit = slots[j : j + 1, :] == wanted
        class_of = class_of + jnp.where(hit, (lane_row + (j * ROWS + 1)).astype(F32), 0.0)
    class_of = jnp.sum(class_of, axis=1, keepdims=True) - 1.0
    member = jnp.where(class_of == lab_lanes, 1.0, 0.0).astype(BF16)
    s_part[...] = dot(member, all_keys()).reshape(2, SIDE, 8, WIDTH)
    s_id = cp.send(s_part.at[other], s_recv, sib)

    for (ref, z_sent), (_, s_sent) in zip(late_z, late_s):
        for o in RING:
            back = SIDE - o
            cp.arrived(ref.at[row(back)], z_sent[o])
            s_sent[back] = cp.send(ref.at[row(back)], ref.at[row(back)], sib)
    cp.finish()

    totals = trow[...]
    for o in t_ids:
        cp.arrived(tz.at[o], t_ids[o])
        totals = totals + tz[o]
    first = lax.broadcasted_iota(jnp.int32, (2 * ROW_BLOCKS, ROWS), 0) < ROW_BLOCKS
    scales = turned(1.0 / jnp.where(first, totals, jnp.maximum(totals - 1.0, 1.0)))
    for k in range(ROW_BLOCKS):
        rows = slice(k * ROWS, (k + 1) * ROWS)
        rinv[rows, :] = scales[:, k : k + 1]
        pinv[rows, :] = 2.0 * scales[:, ROW_BLOCKS + k : ROW_BLOCKS + k + 1]
    col_totals = csum[...]
    for o in PLANE:
        cp.arrived(cz.at[o[0] * SIDE + o[1]], c_ids[o])
        col_totals = col_totals + cz[o[0] * SIDE + o[1]]
    cinv = 1.0 / col_totals
    cinv_lines = [
        jnp.concatenate([cinv[l * SIDE + k : l * SIDE + k + 1, :] for k in range(SIDE)], axis=1)
        for l in range(SIDE)
    ]

    def gradient(rows):
        scale = rinv[rows, :]
        weights = jnp.concatenate(
            [(e[l, rows, :] * (scale + cinv_lines[l])).astype(BF16) for l in range(SIDE)], axis=1
        )
        return dot(weights, all_keys()) - pinv[rows, :] * mu[rows, :]

    def project(part, rows, block, count):
        high = urow[pl.ds(block, count)].astype(F32).reshape(part.shape)
        unit = high + ulow[pl.ds(block, count)].astype(F32).reshape(part.shape)
        radial = jnp.sum(unit * part, axis=1, keepdims=True)
        return (rnorm[rows, :] * (part - unit * radial)).astype(BF16)

    def late_wait(o):
        for ref, s_sent in late_s:
            cp.arrived(ref.at[row_sib(o)], s_sent[o])

    for o in range(SIDE):
        late_wait(o)

    o_ids = []
    for c_, keep in ((other, osib), (c, obuf)):
        for h in range(2):
            first_row = c_ * LINE + h * TILE
            rows = pl.ds(pl.multiple_of(first_row, TILE), TILE)
            half = pl.ds(h * TILE, TILE)
            part = gradient(rows)
            keep[half, :] = part
            if keep is osib:
                o_ids.append(cp.send(osib.at[half], orecv.at[half], sib))
            dpart[rows, :] = project(part, rows, c_ * SIDE + 2 * h, 2)

    def feats(c_, h):
        runs = pl.ds(pl.multiple_of(c_ * LINE + h * TILE, TILE), TILE)
        return jnp.concatenate([frow[k, runs, :] for k in range(ROW_BLOCKS)], axis=1)

    gs_ids = []
    for h in range(2):
        half = pl.ds(h * TILE, TILE)
        g_sib[half] = dot(feats(other, h), dpart[...])
        gs_ids.append(cp.send(g_sib.at[half], g_sib_recv.at[half], sib))
    for h in range(2):
        g_own[pl.ds(2 * h, 2)] = dot(feats(c, h), dpart[...]).reshape(2, SIDE, 4 * 8, WIDTH)

    cp.arrived(s_recv, s_id)
    s_recv[...] = s_recv[...] + s_part[c]
    s_ids = [cp.send(s_recv.at[ring(z, o)], s_zrecv.at[o - 1], z_dev[o]) for o in (1, 2, 3)]

    o_zids = {}
    for h in range(2):
        cp.arrived(orecv.at[pl.ds(h * TILE, TILE)], o_ids[h])

    def rows_of(z_):
        there = pl.ds(pl.multiple_of(z_ * ROWS, ROWS), ROWS)
        return obuf[there, :] + orecv[there, :]

    for o in (2, 1, 3):
        zsend[o - 1] = rows_of(ring(z, o)).astype(BF16)
        o_zids[o] = cp.send(zsend.at[o - 1], zrecv.at[o - 1], z_dev[o])

    for h in range(2):
        half = pl.ds(h * TILE, TILE)
        cp.arrived(g_sib_recv.at[half], gs_ids[h])
        g_own[pl.ds(2 * h, 2)] = g_own[pl.ds(2 * h, 2)] + g_sib_recv[half].reshape(
            2, SIDE, 4 * 8, WIDTH
        )
    g_ids = {}
    for o in PLANE:
        k = o[0] * SIDE + o[1]
        g_send[k] = g_own[ring(x, o[0]), ring(y, o[1])].astype(BF16)
        g_ids[o] = cp.send(g_send.at[k], g_recv.at[k], plane[o])

    for o in (1, 2, 3):
        cp.arrived(s_zrecv.at[o - 1], s_ids[o - 1])
    own_out[...] = (s_recv[z] + s_zrecv[0] + s_zrecv[1] + s_zrecv[2])[0:4, :]
    part = rows_of(z)
    for o in (1, 3, 2):
        cp.arrived(zrecv.at[o - 1], o_zids[o])
        part = part + zrecv[o - 1].astype(F32)
    pg_out[...] = project(part, my_rows, my_row, 1)

    part = g_own[x, y]
    for o in PLANE[::-1]:
        k = o[0] * SIDE + o[1]
        cp.arrived(g_recv.at[k], g_ids[o])
        part = part + g_recv[k].astype(F32)
    g_zsend[...] = part.reshape(SIDE, 8, WIDTH)
    ids = {o: cp.send(g_zsend.at[ring(z, o)], g_zrecv.at[o - 1], z_dev[o]) for o in (2, 1, 3)}
    cp.finish(3)
    part = g_zsend[z]
    for o in (1, 3, 2):
        cp.arrived(g_zrecv.at[o - 1], ids[o])
        part = part + g_zrecv[o - 1]
    wg_out[...] = part

    cp.finish()


def body(features, proj_weight, labels, owner_slot):
    vmem = pl.BlockSpec(memory_space=pltpu.VMEM)
    rows_all = ROW_BLOCKS * ROWS
    scratch = [
        pltpu.VMEM((ROWS, FEATURES), BF16),
        pltpu.VMEM((FEATURES, WIDTH), BF16),
        pltpu.VMEM((COL_BLOCKS, ROWS, WIDTH), BF16),
        pltpu.VMEM((ROW_BLOCKS, ROWS, WIDTH), BF16),
        pltpu.VMEM((ROW_BLOCKS, ROWS, WIDTH), BF16),
        pltpu.VMEM((ROW_BLOCKS, FEATURES, ROWS), BF16),
        pltpu.VMEM((2, SIDE, SIDE, SIDE, 8, ROWS), F32),
        pltpu.VMEM((SIDE, rows_all, LINE), F32),
        pltpu.VMEM((COL_BLOCKS, 1, ROWS), F32),
        pltpu.VMEM((ROW_BLOCKS, 2, ROWS), F32),
        pltpu.VMEM((rows_all, 1), F32),
        pltpu.VMEM((rows_all, 1), F32),
        pltpu.VMEM((rows_all, ROWS), F32),
        pltpu.VMEM((rows_all, 1), F32),
        pltpu.VMEM((rows_all, 1), F32),
        pltpu.VMEM((rows_all, 1), F32),
        pltpu.VMEM((COL_BLOCKS, ROWS), F32),
        pltpu.VMEM((16, COL_BLOCKS, ROWS), F32),
        pltpu.VMEM((2 * ROW_BLOCKS, ROWS), F32),
        pltpu.VMEM((8, 2 * ROW_BLOCKS, ROWS), F32),
        pltpu.VMEM((rows_all, WIDTH), F32),
        pltpu.VMEM((LINE, WIDTH), F32),
        pltpu.VMEM((LINE, WIDTH), F32),
        pltpu.VMEM((LINE, WIDTH), F32),
        pltpu.VMEM((rows_all, WIDTH), BF16),
        pltpu.VMEM((LINE, WIDTH), F32),
        pltpu.VMEM((LINE, WIDTH), F32),
        pltpu.VMEM((3, ROWS, WIDTH), BF16),
        pltpu.VMEM((3, ROWS, WIDTH), BF16),
        pltpu.VMEM((SIDE, SIDE, 4 * 8, WIDTH), F32),
        pltpu.VMEM((16, 4 * 8, WIDTH), BF16),
        pltpu.VMEM((16, 4 * 8, WIDTH), BF16),
        pltpu.VMEM((SIDE, 8, WIDTH), F32),
        pltpu.VMEM((3, 8, WIDTH), F32),
        pltpu.VMEM((2, SIDE, 8, WIDTH), F32),
        pltpu.VMEM((SIDE, 8, WIDTH), F32),
        pltpu.VMEM((3, 8, WIDTH), F32),
        pltpu.SemaphoreType.DMA((N_COPIES,)),
        pltpu.SemaphoreType.DMA((N_COPIES,)),
        pltpu.SemaphoreType.DMA((2,)),
    ]
    return pl.pallas_call(
        kernel,
        out_shape=(
            jax.ShapeDtypeStruct((ROWS, WIDTH), BF16),
            jax.ShapeDtypeStruct((8, WIDTH), F32),
            jax.ShapeDtypeStruct((4, WIDTH), F32),
        ),
        in_specs=[pl.BlockSpec(memory_space=pl.ANY)] * 2 + [vmem] * 2,
        out_specs=(vmem,) * 3,
        scratch_shapes=scratch,
        compiler_params=pltpu.CompilerParams(
            collective_id=0, has_side_effects=True, vmem_limit_bytes=56 * 1024 * 1024
        ),
        name="contrastive",
    )(features, proj_weight, labels.reshape(1, ROWS), owner_slot.reshape(CLASSES // ROWS, ROWS))


def solution(mesh):
    in_specs = (P(("dp", "grp"), None), P(), P(("dp", "grp")), P())
    out_specs = (P(("dp", "grp"), None), P(("dp", "grp"), None), P(("dp", "grp"), None))
    return jax.shard_map(body, mesh=mesh, in_specs=in_specs, out_specs=out_specs, check_vma=False)
```

```python
import jax
import jax.numpy as jnp
from jax import lax
from jax.experimental import pallas as pl
from jax.experimental.pallas import tpu as pltpu
from jax.sharding import PartitionSpec as P

MESH = pl.DeviceIdType.MESH
SIDE = 4
ROWS = 128
FEATURES = 1024
WIDTH = 512
CLASSES = 512
ROW_BLOCKS = 8
COL_BLOCKS = 16
LINE = SIDE * ROWS
N_COPIES = 120
RING = (1, 3, 2)
PLANE = tuple(sorted(((a, b) for a in range(4) for b in range(4) if a or b), key=lambda o: -(min(o[0], 4 - o[0]) + min(o[1], 4 - o[1]))))
INV_SHARPNESS = 10.0
LOG2_SCALE = 14.426950408889634
F32 = jnp.float32
BF16 = jnp.bfloat16


def dot(a, b):
    return jnp.dot(a, b, preferred_element_type=F32)


def dot_nt(a, b):
    return lax.dot_general(a, b, (((1,), (1,)), ((), ())), preferred_element_type=F32)


class Copies:
    def __init__(self, send_sems, recv_sems, any_device):
        self.send_sems, self.recv_sems, self.any_device = send_sems, recv_sems, any_device
        self.used = 0
        self.started = []

    def _copy(self, src, dst, k, device):
        return pltpu.make_async_remote_copy(
            src_ref=src,
            dst_ref=dst,
            send_sem=self.send_sems.at[k],
            recv_sem=self.recv_sems.at[k],
            device_id=device,
            device_id_type=MESH,
        )

    def send(self, src, dst, device):
        k = self.used
        self.used += 1
        copy = self._copy(src, dst, k, device)
        copy.start()
        self.started.append(copy)
        return k

    def arrived(self, dst, k):
        self._copy(dst, dst, k, self.any_device).wait_recv()

    def finish(self, keep=0):
        done = len(self.started) - keep
        for copy in self.started[:done]:
            copy.wait_send()
        self.started = self.started[done:]


def kernel(
    feat_hbm,
    wgt_hbm,
    lab,
    slots,
    pg_out,
    wg_out,
    own_out,
    feat,
    wgt,
    ucol,
    urow,
    ulow,
    frow,
    feat_t,
    e,
    lcol,
    lrow,
    rlab,
    rnorm,
    racc,
    rcnt,
    rinv,
    pinv,
    csum,
    cz,
    trow,
    tz,
    mu,
    osib,
    orecv,
    obuf,
    dpart,
    g_sib,
    g_sib_recv,
    zsend,
    zrecv,
    g_own,
    g_send,
    g_recv,
    g_zsend,
    g_zrecv,
    s_part,
    s_recv,
    s_zrecv,
    send_sems,
    recv_sems,
    load_sems,
):
    dp = lax.axis_index("dp")
    y = lax.axis_index("grp")
    c = lax.rem(dp, 2)
    x = lax.rem(lax.div(dp, 2), SIDE)
    z = lax.div(dp, 2 * SIDE)
    other = 1 - c
    p = other * x + c * y
    q = other * y + c * x

    def ring(v, o):
        return lax.rem(v + o, SIDE)

    def at(z_, x_, c_, y_):
        return ((z_ * SIDE + x_) * 2 + c_, y_)

    def at_pq(p_, q_):
        return at(z, other * p_ + c * q_, c, other * q_ + c * p_)

    sib = at(z, x, other, y)
    p_dev = [None] + [at_pq(ring(p, o), q) for o in (1, 2, 3)]
    q_dev = [None] + [at_pq(p, ring(q, o)) for o in (1, 2, 3)]
    z_dev = [None] + [at(ring(z, o), x, c, y) for o in (1, 2, 3)]
    z_sib = [sib] + [at(ring(z, o), x, other, y) for o in (1, 2, 3)]
    plane = {(a, b): at(z, ring(x, a), c, ring(y, b)) for a, b in PLANE}
    peers = p_dev[1:] + q_dev[1:] + z_dev[1:] + [sib]

    barrier = pltpu.get_barrier_semaphore()
    for peer in peers:
        pl.semaphore_signal(barrier, inc=1, device_id=peer, device_id_type=MESH)

    cp = Copies(send_sems, recv_sems, sib)
    my_col = q * SIDE + p
    my_row = c * SIDE + z

    loads = [
        pltpu.make_async_copy(feat_hbm, feat, load_sems.at[0]),
        pltpu.make_async_copy(wgt_hbm, wgt, load_sems.at[1]),
    ]
    for load in loads:
        load.start()
    for load in loads:
        load.wait()

    projected = dot(feat[...], wgt[...])
    inv_norm = lax.rsqrt(jnp.sum(projected * projected, axis=1, keepdims=True) + 1e-06)
    unit = projected * inv_norm
    u16 = unit.astype(BF16)
    ulow[my_row] = (unit - u16.astype(F32)).astype(BF16)
    ucol[my_col] = u16
    urow[my_row] = u16
    my_lab = lab[...].astype(F32)
    lcol[my_col] = my_lab
    inv_lanes = jnp.transpose(jnp.broadcast_to(inv_norm, (ROWS, ROWS)))[0:1, :]
    lrow[my_row] = jnp.concatenate([my_lab, inv_lanes], axis=0)

    pl.semaphore_wait(barrier, len(peers))

    lab_p = {o: cp.send(lcol.at[my_col], lcol.at[my_col], p_dev[o]) for o in RING}
    lab_z = {o: cp.send(lrow.at[my_row], lrow.at[my_row], z_dev[o]) for o in RING}

    def col(o_p, o_q):
        return ring(q, o_q) * SIDE + ring(p, o_p)

    def row(o_z):
        return c * SIDE + ring(z, o_z)

    def row_sib(o_z):
        return other * SIDE + ring(z, o_z)

    def spread(ref, slot, devs, offsets=RING):
        return {o: cp.send(ref.at[slot], ref.at[slot], devs[o]) for o in offsets}

    p_ids = spread(ucol, my_col, p_dev, (1, 3))
    first_sent, cp.started = cp.started[-2:], cp.started[:-2]
    z_ids = spread(urow, my_row, z_dev)
    sib_ids = {0: cp.send(urow.at[my_row], urow.at[my_row], sib)}
    for copy in first_sent:
        copy.wait_send()
    p_ids.update(spread(ucol, my_col, p_dev, (2,)))
    q_ids = {0: spread(ucol, my_col, q_dev, (1, 3))}
    late_z = [(ulow, spread(ulow, my_row, z_dev))]

    turn = jnp.transpose(feat[...].astype(F32)).reshape(SIDE, SIDE, 2, SIDE, 8, ROWS)
    for z_ in range(SIDE):
        for x_ in range(SIDE):
            for c_ in range(2):
                for y_ in range(SIDE):
                    feat_t[c_, x_, y_, z_] = turn[z_, x_, c_, y_]
    frow[my_row] = feat_t[...].reshape(FEATURES, ROWS).astype(BF16)
    late_z.append((frow, spread(frow, my_row, z_dev)))

    for o in RING:
        cp.arrived(lcol.at[col(SIDE - o, 0)], lab_p[o])
        cp.arrived(lrow.at[row(SIDE - o)], lab_z[o])
    my_line = lcol.at[pl.ds(q * SIDE, SIDE)]
    lab_q = {o: cp.send(my_line, my_line, q_dev[o]) for o in RING}
    my_set = lrow.at[pl.ds(c * SIDE, SIDE)]
    lab_s = cp.send(my_set, my_set, sib)

    for o in (1, 3):
        back = SIDE - o
        cp.arrived(ucol.at[col(back, 0)], p_ids[o])
        q_ids[back] = spread(ucol, col(back, 0), q_dev, (1, 3))
    q_ids[0].update(spread(ucol, my_col, q_dev, (2,)))
    for back in (3, 1):
        q_ids[back].update(spread(ucol, col(back, 0), q_dev, (2,)))
    cp.arrived(ucol.at[col(2, 0)], p_ids[2])
    q_ids[2] = spread(ucol, col(2, 0), q_dev)
    for o in RING:
        back = SIDE - o
        cp.arrived(urow.at[row(back)], z_ids[o])
        sib_ids[back] = cp.send(urow.at[row(back)], urow.at[row(back)], sib)

    late_s = [(ref, {0: cp.send(ref.at[my_row], ref.at[my_row], sib)}) for ref in (ulow, frow)]

    for o in RING:
        line = lcol.at[pl.ds(ring(q, SIDE - o) * SIDE, SIDE)]
        cp.arrived(line, lab_q[o])
    cp.arrived(lrow.at[pl.ds(other * SIDE, SIDE)], lab_s)

    lane = lax.broadcasted_iota(jnp.int32, (ROWS, ROWS), 1)

    def turned(block):
        pad = jnp.zeros((ROWS - block.shape[0], ROWS), F32)
        return jnp.transpose(jnp.concatenate([block, pad], axis=0))

    lab_t = turned(jnp.concatenate([lrow[k] for k in range(ROW_BLOCKS)], axis=0))
    for k in range(ROW_BLOCKS):
        rlab[k * ROWS : (k + 1) * ROWS, :] = lab_t[:, 2 * k : 2 * k + 1]
        rnorm[k * ROWS : (k + 1) * ROWS, :] = lab_t[:, 2 * k + 1 : 2 * k + 2] * INV_SHARPNESS

    def count_block(k, carry):
        rows = pl.ds(pl.multiple_of(k * ROWS, ROWS), ROWS)
        mine = rlab[rows, :]
        total = jnp.zeros((ROWS, ROWS), F32)
        for j in range(COL_BLOCKS):
            total = total + jnp.where(mine == lcol[j], 1.0, 0.0)
        rcnt[rows, :] = jnp.sum(total, axis=1, keepdims=True)
        racc[rows, :] = jnp.zeros((ROWS, ROWS), F32)
        return carry

    lax.fori_loop(0, ROW_BLOCKS, count_block, 0)

    for o in (0, 3, 1, 2):
        cp.arrived(urow.at[row_sib(o)], sib_ids[o])

    TILE = 256

    def line_tiles(q_, own_line):
        keys = ucol[pl.ds(q_ * SIDE, SIDE)].reshape(LINE, WIDTH)
        queries = urow[...].reshape(ROW_BLOCKS * ROWS, WIDTH)
        value = jnp.exp2(dot_nt(queries, keys) * LOG2_SCALE)
        if own_line:
            i = lax.broadcasted_iota(jnp.int32, value.shape, 0) - my_row * ROWS
            j = lax.broadcasted_iota(jnp.int32, value.shape, 1) - p * ROWS
            value = jnp.where((i == j) & (j >= 0) & (j < ROWS), 0.0, value)
        e[q_] = value
        racc[...] += (
            value[:, 0:ROWS]
            + value[:, ROWS : 2 * ROWS]
            + value[:, 2 * ROWS : 3 * ROWS]
            + value[:, 3 * ROWS : 4 * ROWS]
        )
        return jnp.sum(value.reshape(ROW_BLOCKS * ROWS // 8, 8, LINE), axis=0)

    def put_sums(q_, sums):
        total = jnp.sum(sums, axis=0, keepdims=True)
        for k in range(SIDE):
            csum[pl.ds(q_ * SIDE + k, 1), :] = total[:, k * ROWS : (k + 1) * ROWS]

    put_sums(q, line_tiles(q, True))
    for o in RING:
        for o_p in (0, 3, 1, 2):
            cp.arrived(ucol.at[col(o_p, SIDE - o)], q_ids[o_p][o])
        q_ = ring(q, SIDE - o)
        put_sums(q_, line_tiles(q_, False))

    c_ids = {o: cp.send(csum, cz.at[o[0] * SIDE + o[1]], plane[o]) for o in PLANE}
    table = jnp.zeros((ROWS, ROWS), F32)
    for k in range(ROW_BLOCKS):
        rows = slice(k * ROWS, (k + 1) * ROWS)
        table = jnp.where(lane == k, jnp.sum(racc[rows, :], axis=1, keepdims=True), table)
        table = jnp.where(lane == ROW_BLOCKS + k, rcnt[rows, :], table)
    trow[...] = jnp.transpose(table)[0 : 2 * ROW_BLOCKS, :]
    t_ids = {}
    for o in RING:
        t_ids[o] = cp.send(trow, tz.at[o], z_dev[o])
        t_ids[4 + o] = cp.send(trow, tz.at[4 + o], z_sib[o])
    t_ids[4] = cp.send(trow, tz.at[4], sib)

    lab_lanes = jnp.concatenate([lcol[j] for j in range(COL_BLOCKS)], axis=1)

    def all_keys():
        return ucol[...].reshape(COL_BLOCKS * ROWS, WIDTH)

    def class_tile(r, carry):
        rows = pl.ds(pl.multiple_of(r * TILE, TILE), TILE)
        same = jnp.where(rlab[rows, :] == lab_lanes, 1.0, 0.0).astype(BF16)
        mu[rows, :] = dot(same, all_keys())
        return carry

    lax.fori_loop(0, 4, class_tile, 0)
    my_rows = pl.ds(pl.multiple_of(my_row * ROWS, ROWS), ROWS)
    mu[my_rows, :] = mu[my_rows, :] - urow[my_row].astype(F32)

    rho = lax.broadcasted_iota(jnp.int32, (8 * ROW_BLOCKS, 1), 0)
    block, k_slot = rho // 8, rho % 8
    owner = (((block % SIDE) * SIDE + x) * 2 + block // SIDE) * SIDE + y
    wanted = jnp.where(k_slot < 4, owner * 4 + k_slot, -1)
    class_of = jnp.zeros((8 * ROW_BLOCKS, ROWS), F32)
    lane_row = lax.broadcasted_iota(jnp.int32, (8 * ROW_BLOCKS, ROWS), 1)
    for j in range(CLASSES // ROWS):
        hit = slots[j : j + 1, :] == wanted
        class_of = class_of + jnp.where(hit, (lane_row + (j * ROWS + 1)).astype(F32), 0.0)
    class_of = jnp.sum(class_of, axis=1, keepdims=True) - 1.0
    member = jnp.where(class_of == lab_lanes, 1.0, 0.0).astype(BF16)
    s_part[...] = dot(member, all_keys()).reshape(2, SIDE, 8, WIDTH)
    s_id = cp.send(s_part.at[other], s_recv, sib)

    for (ref, z_sent), (_, s_sent) in zip(late_z, late_s):
        for o in RING:
            back = SIDE - o
            cp.arrived(ref.at[row(back)], z_sent[o])
            s_sent[back] = cp.send(ref.at[row(back)], ref.at[row(back)], sib)
    cp.finish()

    totals = trow[...]
    for o in t_ids:
        cp.arrived(tz.at[o], t_ids[o])
        totals = totals + tz[o]
    first = lax.broadcasted_iota(jnp.int32, (2 * ROW_BLOCKS, ROWS), 0) < ROW_BLOCKS
    scales = turned(1.0 / jnp.where(first, totals, jnp.maximum(totals - 1.0, 1.0)))
    for k in range(ROW_BLOCKS):
        rows = slice(k * ROWS, (k + 1) * ROWS)
        rinv[rows, :] = scales[:, k : k + 1]
        pinv[rows, :] = 2.0 * scales[:, ROW_BLOCKS + k : ROW_BLOCKS + k + 1]
    col_totals = csum[...]
    for o in PLANE:
        cp.arrived(cz.at[o[0] * SIDE + o[1]], c_ids[o])
        col_totals = col_totals + cz[o[0] * SIDE + o[1]]
    cinv = 1.0 / col_totals
    cinv_lines = [
        jnp.concatenate([cinv[l * SIDE + k : l * SIDE + k + 1, :] for k in range(SIDE)], axis=1)
        for l in range(SIDE)
    ]

    def gradient(rows):
        scale = rinv[rows, :]
        weights = jnp.concatenate(
            [(e[l, rows, :] * (scale + cinv_lines[l])).astype(BF16) for l in range(SIDE)], axis=1
        )
        return dot(weights, all_keys()) - pinv[rows, :] * mu[rows, :]

    def project(part, rows, block, count):
        high = urow[pl.ds(block, count)].astype(F32).reshape(part.shape)
        unit = high + ulow[pl.ds(block, count)].astype(F32).reshape(part.shape)
        radial = jnp.sum(unit * part, axis=1, keepdims=True)
        return (rnorm[rows, :] * (part - unit * radial)).astype(BF16)

    def late_wait(o):
        for ref, s_sent in late_s:
            cp.arrived(ref.at[row_sib(o)], s_sent[o])

    for o in range(SIDE):
        late_wait(o)

    for c_, keep in ((other, osib), (c, obuf)):
        rows = pl.ds(pl.multiple_of(c_ * LINE, LINE), LINE)
        part = gradient(rows)
        keep[...] = part
        if keep is osib:
            o_id = cp.send(osib, orecv, sib)
        dpart[rows, :] = project(part, rows, c_ * SIDE, SIDE)

    def feats(c_, h):
        runs = pl.ds(pl.multiple_of(c_ * LINE + h * TILE, TILE), TILE)
        return jnp.concatenate([frow[k, runs, :] for k in range(ROW_BLOCKS)], axis=1)

    gs_ids = []
    for h in range(2):
        half = pl.ds(h * TILE, TILE)
        g_sib[half] = dot(feats(other, h), dpart[...])
        gs_ids.append(cp.send(g_sib.at[half], g_sib_recv.at[half], sib))
    for h in range(2):
        g_own[pl.ds(2 * h, 2)] = dot(feats(c, h), dpart[...]).reshape(2, SIDE, 4 * 8, WIDTH)

    cp.arrived(s_recv, s_id)
    s_recv[...] = s_recv[...] + s_part[c]
    s_ids = [cp.send(s_recv.at[ring(z, o)], s_zrecv.at[o - 1], z_dev[o]) for o in (1, 2, 3)]

    o_zids = {}
    cp.arrived(orecv, o_id)

    def rows_of(z_):
        there = pl.ds(pl.multiple_of(z_ * ROWS, ROWS), ROWS)
        return obuf[there, :] + orecv[there, :]

    for o in (2, 1, 3):
        zsend[o - 1] = rows_of(ring(z, o)).astype(BF16)
        o_zids[o] = cp.send(zsend.at[o - 1], zrecv.at[o - 1], z_dev[o])

    for h in range(2):
        cp.arrived(g_sib_recv.at[pl.ds(h * TILE, TILE)], gs_ids[h])

    def g_rows(x_, y_):
        runs = pl.ds(pl.multiple_of((x_ * SIDE + y_) * 32, 32), 32)
        return g_own[x_, y_] + g_sib_recv[runs, :]

    g_ids = {}
    for o in PLANE:
        k = o[0] * SIDE + o[1]
        g_send[k] = g_rows(ring(x, o[0]), ring(y, o[1])).astype(BF16)
        g_ids[o] = cp.send(g_send.at[k], g_recv.at[k], plane[o])

    for o in (1, 2, 3):
        cp.arrived(s_zrecv.at[o - 1], s_ids[o - 1])
    own_out[...] = (s_recv[z] + s_zrecv[0] + s_zrecv[1] + s_zrecv[2])[0:4, :]
    part = rows_of(z)
    for o in (1, 3, 2):
        cp.arrived(zrecv.at[o - 1], o_zids[o])
        part = part + zrecv[o - 1].astype(F32)
    pg_out[...] = project(part, my_rows, my_row, 1)

    part = g_rows(x, y)
    for o in PLANE[::-1]:
        k = o[0] * SIDE + o[1]
        cp.arrived(g_recv.at[k], g_ids[o])
        part = part + g_recv[k].astype(F32)
    g_zsend[...] = part.reshape(SIDE, 8, WIDTH)
    ids = {o: cp.send(g_zsend.at[ring(z, o)], g_zrecv.at[o - 1], z_dev[o]) for o in (2, 1, 3)}
    cp.finish(3)
    part = g_zsend[z]
    for o in (1, 3, 2):
        cp.arrived(g_zrecv.at[o - 1], ids[o])
        part = part + g_zrecv[o - 1]
    wg_out[...] = part

    cp.finish()


def body(features, proj_weight, labels, owner_slot):
    vmem = pl.BlockSpec(memory_space=pltpu.VMEM)
    rows_all = ROW_BLOCKS * ROWS
    scratch = [
        pltpu.VMEM((ROWS, FEATURES), BF16),
        pltpu.VMEM((FEATURES, WIDTH), BF16),
        pltpu.VMEM((COL_BLOCKS, ROWS, WIDTH), BF16),
        pltpu.VMEM((ROW_BLOCKS, ROWS, WIDTH), BF16),
        pltpu.VMEM((ROW_BLOCKS, ROWS, WIDTH), BF16),
        pltpu.VMEM((ROW_BLOCKS, FEATURES, ROWS), BF16),
        pltpu.VMEM((2, SIDE, SIDE, SIDE, 8, ROWS), F32),
        pltpu.VMEM((SIDE, rows_all, LINE), F32),
        pltpu.VMEM((COL_BLOCKS, 1, ROWS), F32),
        pltpu.VMEM((ROW_BLOCKS, 2, ROWS), F32),
        pltpu.VMEM((rows_all, 1), F32),
        pltpu.VMEM((rows_all, 1), F32),
        pltpu.VMEM((rows_all, ROWS), F32),
        pltpu.VMEM((rows_all, 1), F32),
        pltpu.VMEM((rows_all, 1), F32),
        pltpu.VMEM((rows_all, 1), F32),
        pltpu.VMEM((COL_BLOCKS, ROWS), F32),
        pltpu.VMEM((16, COL_BLOCKS, ROWS), F32),
        pltpu.VMEM((2 * ROW_BLOCKS, ROWS), F32),
        pltpu.VMEM((8, 2 * ROW_BLOCKS, ROWS), F32),
        pltpu.VMEM((rows_all, WIDTH), F32),
        pltpu.VMEM((LINE, WIDTH), F32),
        pltpu.VMEM((LINE, WIDTH), F32),
        pltpu.VMEM((LINE, WIDTH), F32),
        pltpu.VMEM((rows_all, WIDTH), BF16),
        pltpu.VMEM((LINE, WIDTH), F32),
        pltpu.VMEM((LINE, WIDTH), F32),
        pltpu.VMEM((3, ROWS, WIDTH), BF16),
        pltpu.VMEM((3, ROWS, WIDTH), BF16),
        pltpu.VMEM((SIDE, SIDE, 4 * 8, WIDTH), F32),
        pltpu.VMEM((16, 4 * 8, WIDTH), BF16),
        pltpu.VMEM((16, 4 * 8, WIDTH), BF16),
        pltpu.VMEM((SIDE, 8, WIDTH), F32),
        pltpu.VMEM((3, 8, WIDTH), F32),
        pltpu.VMEM((2, SIDE, 8, WIDTH), F32),
        pltpu.VMEM((SIDE, 8, WIDTH), F32),
        pltpu.VMEM((3, 8, WIDTH), F32),
        pltpu.SemaphoreType.DMA((N_COPIES,)),
        pltpu.SemaphoreType.DMA((N_COPIES,)),
        pltpu.SemaphoreType.DMA((2,)),
    ]
    return pl.pallas_call(
        kernel,
        out_shape=(
            pltpu.VMEM((ROWS, WIDTH), BF16),
            pltpu.VMEM((8, WIDTH), F32),
            pltpu.VMEM((4, WIDTH), F32),
        ),
        in_specs=[pl.BlockSpec(memory_space=pl.ANY)] * 2 + [vmem] * 2,
        out_specs=(vmem,) * 3,
        scratch_shapes=scratch,
        compiler_params=pltpu.CompilerParams(
            collective_id=0, has_side_effects=True, vmem_limit_bytes=56 * 1024 * 1024
        ),
        name="contrastive",
    )(features, proj_weight, labels.reshape(1, ROWS), owner_slot.reshape(CLASSES // ROWS, ROWS))


def solution(mesh):
    in_specs = (P(("dp", "grp"), None), P(), P(("dp", "grp")), P())
    out_specs = (P(("dp", "grp"), None), P(("dp", "grp"), None), P(("dp", "grp"), None))
    return jax.shard_map(body, mesh=mesh, in_specs=in_specs, out_specs=out_specs, check_vma=False)
```

```python
import jax
import jax.numpy as jnp
from jax import lax
from jax.experimental import pallas as pl
from jax.experimental.pallas import tpu as pltpu
from jax.sharding import PartitionSpec as P

MESH = pl.DeviceIdType.MESH
SIDE = 4
ROWS = 128
FEATURES = 1024
WIDTH = 512
CLASSES = 512
ROW_BLOCKS = 8
COL_BLOCKS = 16
LINE = SIDE * ROWS
N_COPIES = 120
RING = (1, 3, 2)
PLANE = tuple(sorted(((a, b) for a in range(4) for b in range(4) if a or b), key=lambda o: -(min(o[0], 4 - o[0]) + min(o[1], 4 - o[1]))))
INV_SHARPNESS = 10.0
LOG2_SCALE = 14.426950408889634
F32 = jnp.float32
BF16 = jnp.bfloat16


def dot(a, b):
    return jnp.dot(a, b, preferred_element_type=F32)


def dot_nt(a, b):
    return lax.dot_general(a, b, (((1,), (1,)), ((), ())), preferred_element_type=F32)


class Copies:
    def __init__(self, send_sems, recv_sems, any_device):
        self.send_sems, self.recv_sems, self.any_device = send_sems, recv_sems, any_device
        self.used = 0
        self.started = []

    def _copy(self, src, dst, k, device):
        return pltpu.make_async_remote_copy(
            src_ref=src,
            dst_ref=dst,
            send_sem=self.send_sems.at[k],
            recv_sem=self.recv_sems.at[k],
            device_id=device,
            device_id_type=MESH,
        )

    def send(self, src, dst, device):
        k = self.used
        self.used += 1
        copy = self._copy(src, dst, k, device)
        copy.start()
        self.started.append(copy)
        return k

    def arrived(self, dst, k):
        self._copy(dst, dst, k, self.any_device).wait_recv()

    def finish(self, keep=0):
        done = len(self.started) - keep
        for copy in self.started[:done]:
            copy.wait_send()
        self.started = self.started[done:]


def kernel(
    feat_hbm,
    wgt_hbm,
    lab,
    slots,
    pg_out,
    wg_out,
    own_out,
    feat,
    wgt,
    ucol,
    urow,
    ulow,
    frow,
    feat_t,
    e,
    lcol,
    lrow,
    rlab,
    rnorm,
    racc,
    rcnt,
    rinv,
    pinv,
    csum,
    cz,
    trow,
    tz,
    mu,
    osib,
    orecv,
    obuf,
    dpart,
    g_sib,
    g_sib_recv,
    zsend,
    zrecv,
    g_own,
    g_send,
    g_recv,
    g_zsend,
    g_zrecv,
    s_part,
    s_recv,
    s_zrecv,
    send_sems,
    recv_sems,
    load_sems,
):
    dp = lax.axis_index("dp")
    y = lax.axis_index("grp")
    c = lax.rem(dp, 2)
    x = lax.rem(lax.div(dp, 2), SIDE)
    z = lax.div(dp, 2 * SIDE)
    other = 1 - c
    p = other * x + c * y
    q = other * y + c * x

    def ring(v, o):
        return lax.rem(v + o, SIDE)

    def at(z_, x_, c_, y_):
        return ((z_ * SIDE + x_) * 2 + c_, y_)

    def at_pq(p_, q_):
        return at(z, other * p_ + c * q_, c, other * q_ + c * p_)

    sib = at(z, x, other, y)
    p_dev = [None] + [at_pq(ring(p, o), q) for o in (1, 2, 3)]
    q_dev = [None] + [at_pq(p, ring(q, o)) for o in (1, 2, 3)]
    z_dev = [None] + [at(ring(z, o), x, c, y) for o in (1, 2, 3)]
    z_sib = [sib] + [at(ring(z, o), x, other, y) for o in (1, 2, 3)]
    plane = {(a, b): at(z, ring(x, a), c, ring(y, b)) for a, b in PLANE}
    peers = p_dev[1:] + q_dev[1:] + z_dev[1:] + [sib]

    barrier = pltpu.get_barrier_semaphore()
    for peer in peers:
        pl.semaphore_signal(barrier, inc=1, device_id=peer, device_id_type=MESH)

    cp = Copies(send_sems, recv_sems, sib)
    my_col = q * SIDE + p
    my_row = c * SIDE + z

    loads = [
        pltpu.make_async_copy(feat_hbm, feat, load_sems.at[0]),
        pltpu.make_async_copy(wgt_hbm, wgt, load_sems.at[1]),
    ]
    for load in loads:
        load.start()
    for load in loads:
        load.wait()

    projected = dot(feat[...], wgt[...])
    inv_norm = lax.rsqrt(jnp.sum(projected * projected, axis=1, keepdims=True) + 1e-06)
    unit = projected * inv_norm
    u16 = unit.astype(BF16)
    ulow[my_row] = (unit - u16.astype(F32)).astype(BF16)
    ucol[my_col] = u16
    urow[my_row] = u16
    my_lab = lab[...].astype(F32)
    lcol[my_col] = my_lab
    inv_lanes = jnp.transpose(jnp.broadcast_to(inv_norm, (ROWS, ROWS)))[0:1, :]
    lrow[my_row] = jnp.concatenate([my_lab, inv_lanes], axis=0)

    pl.semaphore_wait(barrier, len(peers))

    lab_p = {o: cp.send(lcol.at[my_col], lcol.at[my_col], p_dev[o]) for o in RING}
    lab_z = {o: cp.send(lrow.at[my_row], lrow.at[my_row], z_dev[o]) for o in RING}

    def col(o_p, o_q):
        return ring(q, o_q) * SIDE + ring(p, o_p)

    def row(o_z):
        return c * SIDE + ring(z, o_z)

    def row_sib(o_z):
        return other * SIDE + ring(z, o_z)

    def spread(ref, slot, devs, offsets=RING):
        return {o: cp.send(ref.at[slot], ref.at[slot], devs[o]) for o in offsets}

    p_ids = spread(ucol, my_col, p_dev, (1, 3))
    first_sent, cp.started = cp.started[-2:], cp.started[:-2]
    z_ids = spread(urow, my_row, z_dev)
    sib_ids = {0: cp.send(urow.at[my_row], urow.at[my_row], sib)}
    for copy in first_sent:
        copy.wait_send()
    p_ids.update(spread(ucol, my_col, p_dev, (2,)))
    q_ids = {0: spread(ucol, my_col, q_dev, (1, 3))}
    late_z = [(ulow, spread(ulow, my_row, z_dev, (1, 3)))]

    turn = jnp.transpose(feat[...].astype(F32)).reshape(SIDE, SIDE, 2, SIDE, 8, ROWS)
    for z_ in range(SIDE):
        for x_ in range(SIDE):
            for c_ in range(2):
                for y_ in range(SIDE):
                    feat_t[c_, x_, y_, z_] = turn[z_, x_, c_, y_]
    frow[my_row] = feat_t[...].reshape(FEATURES, ROWS).astype(BF16)
    late_z.append((frow, spread(frow, my_row, z_dev, (1, 3))))

    for o in RING:
        cp.arrived(lcol.at[col(SIDE - o, 0)], lab_p[o])
        cp.arrived(lrow.at[row(SIDE - o)], lab_z[o])
    my_line = lcol.at[pl.ds(q * SIDE, SIDE)]
    lab_q = {o: cp.send(my_line, my_line, q_dev[o]) for o in RING}
    my_set = lrow.at[pl.ds(c * SIDE, SIDE)]
    lab_s = cp.send(my_set, my_set, sib)

    for o in (1, 3):
        back = SIDE - o
        cp.arrived(ucol.at[col(back, 0)], p_ids[o])
        q_ids[back] = spread(ucol, col(back, 0), q_dev, (1, 3))
    cp.arrived(ucol.at[col(2, 0)], p_ids[2])
    q_ids[2] = spread(ucol, col(2, 0), q_dev, (2, 1, 3))
    low, high = pl.ds(0, ROWS // 2), pl.ds(ROWS // 2, ROWS // 2)
    far_ids = {}

    def pass_on(o_p):
        before, after = col(o_p, 3), col(o_p, 1)
        cp.arrived(ucol.at[before], q_ids[o_p][1])
        up = cp.send(ucol.at[before, low], ucol.at[before, low], q_dev[1])
        cp.arrived(ucol.at[after], q_ids[o_p][3])
        down = cp.send(ucol.at[after, high], ucol.at[after, high], q_dev[3])
        far_ids[o_p] = (up, down)

    for o in RING:
        back = SIDE - o
        cp.arrived(urow.at[row(back)], z_ids[o])
        sib_ids[back] = cp.send(urow.at[row(back)], urow.at[row(back)], sib)

    late_s = [(ref, {0: cp.send(ref.at[my_row], ref.at[my_row], sib)}) for ref in (ulow, frow)]

    for o in RING:
        line = lcol.at[pl.ds(ring(q, SIDE - o) * SIDE, SIDE)]
        cp.arrived(line, lab_q[o])
    cp.arrived(lrow.at[pl.ds(other * SIDE, SIDE)], lab_s)

    pass_on(0)

    lane = lax.broadcasted_iota(jnp.int32, (ROWS, ROWS), 1)

    def turned(block):
        pad = jnp.zeros((ROWS - block.shape[0], ROWS), F32)
        return jnp.transpose(jnp.concatenate([block, pad], axis=0))

    lab_t = turned(jnp.concatenate([lrow[k] for k in range(ROW_BLOCKS)], axis=0))
    for k in range(ROW_BLOCKS):
        rlab[k * ROWS : (k + 1) * ROWS, :] = lab_t[:, 2 * k : 2 * k + 1]
        rnorm[k * ROWS : (k + 1) * ROWS, :] = lab_t[:, 2 * k + 1 : 2 * k + 2] * INV_SHARPNESS

    def count_block(k, carry):
        rows = pl.ds(pl.multiple_of(k * ROWS, ROWS), ROWS)
        mine = rlab[rows, :]
        total = jnp.zeros((ROWS, ROWS), F32)
        for j in range(COL_BLOCKS):
            total = total + jnp.where(mine == lcol[j], 1.0, 0.0)
        rcnt[rows, :] = jnp.sum(total, axis=1, keepdims=True)
        racc[rows, :] = jnp.zeros((ROWS, ROWS), F32)
        return carry

    lax.fori_loop(0, ROW_BLOCKS, count_block, 0)
    pass_on(3)
    pass_on(1)

    for o in (0, 3, 1, 2):
        cp.arrived(urow.at[row_sib(o)], sib_ids[o])

    TILE = 256

    def line_tiles(q_, own_line):
        keys = ucol[pl.ds(q_ * SIDE, SIDE)].reshape(LINE, WIDTH)
        queries = urow[...].reshape(ROW_BLOCKS * ROWS, WIDTH)
        value = jnp.exp2(dot_nt(queries, keys) * LOG2_SCALE)
        if own_line:
            i = lax.broadcasted_iota(jnp.int32, value.shape, 0) - my_row * ROWS
            j = lax.broadcasted_iota(jnp.int32, value.shape, 1) - p * ROWS
            value = jnp.where((i == j) & (j >= 0) & (j < ROWS), 0.0, value)
        e[q_] = value
        racc[...] += (
            value[:, 0:ROWS]
            + value[:, ROWS : 2 * ROWS]
            + value[:, 2 * ROWS : 3 * ROWS]
            + value[:, 3 * ROWS : 4 * ROWS]
        )
        return jnp.sum(value.reshape(ROW_BLOCKS * ROWS // 8, 8, LINE), axis=0)

    def put_sums(q_, sums):
        total = jnp.sum(sums, axis=0, keepdims=True)
        for k in range(SIDE):
            csum[pl.ds(q_ * SIDE + k, 1), :] = total[:, k * ROWS : (k + 1) * ROWS]

    put_sums(q, line_tiles(q, True))

    def ref_halves(ref):
        n = ref.shape[1] // 2
        return pl.ds(0, n), pl.ds(n, n)

    late_far = []
    for (ref, z_sent), (_, s_sent) in zip(late_z, late_s):
        low_part, high_part = ref_halves(ref)
        before, after = row(3), row(1)
        cp.arrived(ref.at[before], z_sent[1])
        up = cp.send(ref.at[before, low_part], ref.at[before, low_part], z_dev[1])
        s_sent[3] = cp.send(ref.at[before], ref.at[before], sib)
        cp.arrived(ref.at[after], z_sent[3])
        down = cp.send(ref.at[after, high_part], ref.at[after, high_part], z_dev[3])
        s_sent[1] = cp.send(ref.at[after], ref.at[after], sib)
        late_far.append((up, down))

    for o in RING:
        if o == 2:
            for o_p in (0, 3, 1):
                far = col(o_p, 2)
                cp.arrived(ucol.at[far, low], far_ids[o_p][0])
                cp.arrived(ucol.at[far, high], far_ids[o_p][1])
        cp.arrived(ucol.at[col(2, SIDE - o)], q_ids[2][o])
        q_ = ring(q, SIDE - o)
        put_sums(q_, line_tiles(q_, False))

    c_ids = {o: cp.send(csum, cz.at[o[0] * SIDE + o[1]], plane[o]) for o in PLANE}
    table = jnp.zeros((ROWS, ROWS), F32)
    for k in range(ROW_BLOCKS):
        rows = slice(k * ROWS, (k + 1) * ROWS)
        table = jnp.where(lane == k, jnp.sum(racc[rows, :], axis=1, keepdims=True), table)
        table = jnp.where(lane == ROW_BLOCKS + k, rcnt[rows, :], table)
    trow[...] = jnp.transpose(table)[0 : 2 * ROW_BLOCKS, :]
    t_ids = {}
    for o in RING:
        t_ids[o] = cp.send(trow, tz.at[o], z_dev[o])
        t_ids[4 + o] = cp.send(trow, tz.at[4 + o], z_sib[o])
    t_ids[4] = cp.send(trow, tz.at[4], sib)

    lab_lanes = jnp.concatenate([lcol[j] for j in range(COL_BLOCKS)], axis=1)

    def all_keys():
        return ucol[...].reshape(COL_BLOCKS * ROWS, WIDTH)

    def class_tile(r, carry):
        rows = pl.ds(pl.multiple_of(r * TILE, TILE), TILE)
        same = jnp.where(rlab[rows, :] == lab_lanes, 1.0, 0.0).astype(BF16)
        mu[rows, :] = dot(same, all_keys())
        return carry

    lax.fori_loop(0, 4, class_tile, 0)
    my_rows = pl.ds(pl.multiple_of(my_row * ROWS, ROWS), ROWS)
    mu[my_rows, :] = mu[my_rows, :] - urow[my_row].astype(F32)

    rho = lax.broadcasted_iota(jnp.int32, (8 * ROW_BLOCKS, 1), 0)
    block, k_slot = rho // 8, rho % 8
    owner = (((block % SIDE) * SIDE + x) * 2 + block // SIDE) * SIDE + y
    wanted = jnp.where(k_slot < 4, owner * 4 + k_slot, -1)
    class_of = jnp.zeros((8 * ROW_BLOCKS, ROWS), F32)
    lane_row = lax.broadcasted_iota(jnp.int32, (8 * ROW_BLOCKS, ROWS), 1)
    for j in range(CLASSES // ROWS):
        hit = slots[j : j + 1, :] == wanted
        class_of = class_of + jnp.where(hit, (lane_row + (j * ROWS + 1)).astype(F32), 0.0)
    class_of = jnp.sum(class_of, axis=1, keepdims=True) - 1.0
    member = jnp.where(class_of == lab_lanes, 1.0, 0.0).astype(BF16)
    s_part[...] = dot(member, all_keys()).reshape(2, SIDE, 8, WIDTH)
    s_id = cp.send(s_part.at[other], s_recv, sib)

    for (ref, s_sent), (up, down) in zip(late_s, late_far):
        low_part, high_part = ref_halves(ref)
        cp.arrived(ref.at[row(2), low_part], up)
        cp.arrived(ref.at[row(2), high_part], down)
        s_sent[2] = cp.send(ref.at[row(2)], ref.at[row(2)], sib)
    cp.finish()

    totals = trow[...]
    for o in t_ids:
        cp.arrived(tz.at[o], t_ids[o])
        totals = totals + tz[o]
    first = lax.broadcasted_iota(jnp.int32, (2 * ROW_BLOCKS, ROWS), 0) < ROW_BLOCKS
    scales = turned(1.0 / jnp.where(first, totals, jnp.maximum(totals - 1.0, 1.0)))
    for k in range(ROW_BLOCKS):
        rows = slice(k * ROWS, (k + 1) * ROWS)
        rinv[rows, :] = scales[:, k : k + 1]
        pinv[rows, :] = 2.0 * scales[:, ROW_BLOCKS + k : ROW_BLOCKS + k + 1]
    col_totals = csum[...]
    for o in PLANE:
        cp.arrived(cz.at[o[0] * SIDE + o[1]], c_ids[o])
        col_totals = col_totals + cz[o[0] * SIDE + o[1]]
    cinv = 1.0 / col_totals
    cinv_lines = [
        jnp.concatenate([cinv[l * SIDE + k : l * SIDE + k + 1, :] for k in range(SIDE)], axis=1)
        for l in range(SIDE)
    ]

    def gradient(rows):
        scale = rinv[rows, :]
        weights = jnp.concatenate(
            [(e[l, rows, :] * (scale + cinv_lines[l])).astype(BF16) for l in range(SIDE)], axis=1
        )
        return dot(weights, all_keys()) - pinv[rows, :] * mu[rows, :]

    def project(part, rows, block, count):
        high = urow[pl.ds(block, count)].astype(F32).reshape(part.shape)
        unit = high + ulow[pl.ds(block, count)].astype(F32).reshape(part.shape)
        radial = jnp.sum(unit * part, axis=1, keepdims=True)
        return (rnorm[rows, :] * (part - unit * radial)).astype(BF16)

    def late_wait(o):
        for ref, s_sent in late_s:
            cp.arrived(ref.at[row_sib(o)], s_sent[o])

    for o in range(SIDE):
        late_wait(o)

    for c_, keep in ((other, osib), (c, obuf)):
        rows = pl.ds(pl.multiple_of(c_ * LINE, LINE), LINE)
        part = gradient(rows)
        keep[...] = part
        if keep is osib:
            o_id = cp.send(osib, orecv, sib)
        dpart[rows, :] = project(part, rows, c_ * SIDE, SIDE)

    def feats(c_, h):
        runs = pl.ds(pl.multiple_of(c_ * LINE + h * TILE, TILE), TILE)
        return jnp.concatenate([frow[k, runs, :] for k in range(ROW_BLOCKS)], axis=1)

    gs_ids = []
    for h in range(2):
        half = pl.ds(h * TILE, TILE)
        g_sib[half] = dot(feats(other, h), dpart[...])
        gs_ids.append(cp.send(g_sib.at[half], g_sib_recv.at[half], sib))
    for h in range(2):
        g_own[pl.ds(2 * h, 2)] = dot(feats(c, h), dpart[...]).reshape(2, SIDE, 4 * 8, WIDTH)

    cp.arrived(s_recv, s_id)
    s_recv[...] = s_recv[...] + s_part[c]
    s_ids = [cp.send(s_recv.at[ring(z, o)], s_zrecv.at[o - 1], z_dev[o]) for o in (1, 2, 3)]

    o_zids = {}
    cp.arrived(orecv, o_id)

    def rows_of(z_):
        there = pl.ds(pl.multiple_of(z_ * ROWS, ROWS), ROWS)
        return obuf[there, :] + orecv[there, :]

    for o in (2, 1, 3):
        zsend[o - 1] = rows_of(ring(z, o)).astype(BF16)
        o_zids[o] = cp.send(zsend.at[o - 1], zrecv.at[o - 1], z_dev[o])

    for h in range(2):
        cp.arrived(g_sib_recv.at[pl.ds(h * TILE, TILE)], gs_ids[h])

    def g_rows(x_, y_):
        runs = pl.ds(pl.multiple_of((x_ * SIDE + y_) * 32, 32), 32)
        return g_own[x_, y_] + g_sib_recv[runs, :]

    g_ids = {}
    for o in PLANE:
        k = o[0] * SIDE + o[1]
        g_send[k] = g_rows(ring(x, o[0]), ring(y, o[1])).astype(BF16)
        g_ids[o] = cp.send(g_send.at[k], g_recv.at[k], plane[o])

    for o in (1, 2, 3):
        cp.arrived(s_zrecv.at[o - 1], s_ids[o - 1])
    own_out[...] = (s_recv[z] + s_zrecv[0] + s_zrecv[1] + s_zrecv[2])[0:4, :]
    part = rows_of(z)
    for o in (1, 3, 2):
        cp.arrived(zrecv.at[o - 1], o_zids[o])
        part = part + zrecv[o - 1].astype(F32)
    pg_out[...] = project(part, my_rows, my_row, 1)

    part = g_rows(x, y)
    for o in PLANE[::-1]:
        k = o[0] * SIDE + o[1]
        cp.arrived(g_recv.at[k], g_ids[o])
        part = part + g_recv[k].astype(F32)
    g_zsend[...] = part.reshape(SIDE, 8, WIDTH)
    ids = {o: cp.send(g_zsend.at[ring(z, o)], g_zrecv.at[o - 1], z_dev[o]) for o in (2, 1, 3)}
    cp.finish(3)
    part = g_zsend[z]
    for o in (1, 3, 2):
        cp.arrived(g_zrecv.at[o - 1], ids[o])
        part = part + g_zrecv[o - 1]
    wg_out[...] = part

    cp.finish()


def body(features, proj_weight, labels, owner_slot):
    vmem = pl.BlockSpec(memory_space=pltpu.VMEM)
    rows_all = ROW_BLOCKS * ROWS
    scratch = [
        pltpu.VMEM((ROWS, FEATURES), BF16),
        pltpu.VMEM((FEATURES, WIDTH), BF16),
        pltpu.VMEM((COL_BLOCKS, ROWS, WIDTH), BF16),
        pltpu.VMEM((ROW_BLOCKS, ROWS, WIDTH), BF16),
        pltpu.VMEM((ROW_BLOCKS, ROWS, WIDTH), BF16),
        pltpu.VMEM((ROW_BLOCKS, FEATURES, ROWS), BF16),
        pltpu.VMEM((2, SIDE, SIDE, SIDE, 8, ROWS), F32),
        pltpu.VMEM((SIDE, rows_all, LINE), F32),
        pltpu.VMEM((COL_BLOCKS, 1, ROWS), F32),
        pltpu.VMEM((ROW_BLOCKS, 2, ROWS), F32),
        pltpu.VMEM((rows_all, 1), F32),
        pltpu.VMEM((rows_all, 1), F32),
        pltpu.VMEM((rows_all, ROWS), F32),
        pltpu.VMEM((rows_all, 1), F32),
        pltpu.VMEM((rows_all, 1), F32),
        pltpu.VMEM((rows_all, 1), F32),
        pltpu.VMEM((COL_BLOCKS, ROWS), F32),
        pltpu.VMEM((16, COL_BLOCKS, ROWS), F32),
        pltpu.VMEM((2 * ROW_BLOCKS, ROWS), F32),
        pltpu.VMEM((8, 2 * ROW_BLOCKS, ROWS), F32),
        pltpu.VMEM((rows_all, WIDTH), F32),
        pltpu.VMEM((LINE, WIDTH), F32),
        pltpu.VMEM((LINE, WIDTH), F32),
        pltpu.VMEM((LINE, WIDTH), F32),
        pltpu.VMEM((rows_all, WIDTH), BF16),
        pltpu.VMEM((LINE, WIDTH), F32),
        pltpu.VMEM((LINE, WIDTH), F32),
        pltpu.VMEM((3, ROWS, WIDTH), BF16),
        pltpu.VMEM((3, ROWS, WIDTH), BF16),
        pltpu.VMEM((SIDE, SIDE, 4 * 8, WIDTH), F32),
        pltpu.VMEM((16, 4 * 8, WIDTH), BF16),
        pltpu.VMEM((16, 4 * 8, WIDTH), BF16),
        pltpu.VMEM((SIDE, 8, WIDTH), F32),
        pltpu.VMEM((3, 8, WIDTH), F32),
        pltpu.VMEM((2, SIDE, 8, WIDTH), F32),
        pltpu.VMEM((SIDE, 8, WIDTH), F32),
        pltpu.VMEM((3, 8, WIDTH), F32),
        pltpu.SemaphoreType.DMA((N_COPIES,)),
        pltpu.SemaphoreType.DMA((N_COPIES,)),
        pltpu.SemaphoreType.DMA((2,)),
    ]
    return pl.pallas_call(
        kernel,
        out_shape=(
            pltpu.VMEM((ROWS, WIDTH), BF16),
            pltpu.VMEM((8, WIDTH), F32),
            pltpu.VMEM((4, WIDTH), F32),
        ),
        in_specs=[pl.BlockSpec(memory_space=pl.ANY)] * 2 + [vmem] * 2,
        out_specs=(vmem,) * 3,
        scratch_shapes=scratch,
        compiler_params=pltpu.CompilerParams(
            collective_id=0, has_side_effects=True, vmem_limit_bytes=56 * 1024 * 1024
        ),
        name="contrastive",
    )(features, proj_weight, labels.reshape(1, ROWS), owner_slot.reshape(CLASSES // ROWS, ROWS))


def solution(mesh):
    in_specs = (P(("dp", "grp"), None), P(), P(("dp", "grp")), P())
    out_specs = (P(("dp", "grp"), None), P(("dp", "grp"), None), P(("dp", "grp"), None))
    return jax.shard_map(body, mesh=mesh, in_specs=in_specs, out_specs=out_specs, check_vma=False)
```

```python
import jax
import jax.numpy as jnp
from jax import lax
from jax.experimental import pallas as pl
from jax.experimental.pallas import tpu as pltpu
from jax.sharding import PartitionSpec as P

MESH = pl.DeviceIdType.MESH
SIDE = 4
ROWS = 128
FEATURES = 1024
WIDTH = 512
CLASSES = 512
ROW_BLOCKS = 8
COL_BLOCKS = 16
LINE = SIDE * ROWS
N_COPIES = 120
RING = (1, 3, 2)
PLANE = tuple(sorted(((a, b) for a in range(4) for b in range(4) if a or b), key=lambda o: -(min(o[0], 4 - o[0]) + min(o[1], 4 - o[1]))))
INV_SHARPNESS = 10.0
LOG2_SCALE = 14.426950408889634
F32 = jnp.float32
BF16 = jnp.bfloat16


def dot(a, b):
    return jnp.dot(a, b, preferred_element_type=F32)


def dot_nt(a, b):
    return lax.dot_general(a, b, (((1,), (1,)), ((), ())), preferred_element_type=F32)


class Copies:
    def __init__(self, send_sems, recv_sems, any_device):
        self.send_sems, self.recv_sems, self.any_device = send_sems, recv_sems, any_device
        self.used = 0
        self.started = []

    def _copy(self, src, dst, k, device):
        return pltpu.make_async_remote_copy(
            src_ref=src,
            dst_ref=dst,
            send_sem=self.send_sems.at[k],
            recv_sem=self.recv_sems.at[k],
            device_id=device,
            device_id_type=MESH,
        )

    def send(self, src, dst, device):
        k = self.used
        self.used += 1
        copy = self._copy(src, dst, k, device)
        copy.start()
        self.started.append(copy)
        return k

    def arrived(self, dst, k):
        self._copy(dst, dst, k, self.any_device).wait_recv()

    def finish(self, keep=0):
        done = len(self.started) - keep
        for copy in self.started[:done]:
            copy.wait_send()
        self.started = self.started[done:]


def kernel(
    feat_hbm,
    wgt_hbm,
    lab_hbm,
    slots_hbm,
    pg_out,
    wg_out,
    own_out,
    feat,
    wgt,
    lab,
    slots,
    ucol,
    urow,
    ulow,
    frow,
    feat_t,
    e,
    lcol,
    lrow,
    rlab,
    rnorm,
    racc,
    rcnt,
    rinv,
    pinv,
    csum,
    cz,
    trow,
    tz,
    mu,
    osib,
    orecv,
    obuf,
    dpart,
    g_sib,
    g_sib_recv,
    zsend,
    zrecv,
    g_own,
    g_send,
    g_recv,
    g_zsend,
    g_zrecv,
    s_part,
    s_recv,
    s_zrecv,
    send_sems,
    recv_sems,
    load_sems,
):
    dp = lax.axis_index("dp")
    y = lax.axis_index("grp")
    c = lax.rem(dp, 2)
    x = lax.rem(lax.div(dp, 2), SIDE)
    z = lax.div(dp, 2 * SIDE)
    other = 1 - c
    p = other * x + c * y
    q = other * y + c * x

    def ring(v, o):
        return lax.rem(v + o, SIDE)

    def at(z_, x_, c_, y_):
        return ((z_ * SIDE + x_) * 2 + c_, y_)

    def at_pq(p_, q_):
        return at(z, other * p_ + c * q_, c, other * q_ + c * p_)

    sib = at(z, x, other, y)
    p_dev = [None] + [at_pq(ring(p, o), q) for o in (1, 2, 3)]
    q_dev = [None] + [at_pq(p, ring(q, o)) for o in (1, 2, 3)]
    z_dev = [None] + [at(ring(z, o), x, c, y) for o in (1, 2, 3)]
    z_sib = [sib] + [at(ring(z, o), x, other, y) for o in (1, 2, 3)]
    plane = {(a, b): at(z, ring(x, a), c, ring(y, b)) for a, b in PLANE}
    peers = p_dev[1:] + q_dev[1:] + z_dev[1:] + [sib]

    barrier = pltpu.get_barrier_semaphore()
    for peer in peers:
        pl.semaphore_signal(barrier, inc=1, device_id=peer, device_id_type=MESH)

    cp = Copies(send_sems, recv_sems, sib)
    my_col = q * SIDE + p
    my_row = c * SIDE + z

    loads = [
        pltpu.make_async_copy(feat_hbm, feat, load_sems.at[0]),
        pltpu.make_async_copy(wgt_hbm, wgt, load_sems.at[1]),
        pltpu.make_async_copy(lab_hbm, lab, load_sems.at[2]),
        pltpu.make_async_copy(slots_hbm, slots, load_sems.at[3]),
    ]
    for load in loads:
        load.start()
    for load in loads:
        load.wait()

    projected = dot(feat[...], wgt[...])
    inv_norm = lax.rsqrt(jnp.sum(projected * projected, axis=1, keepdims=True) + 1e-06)
    unit = projected * inv_norm
    u16 = unit.astype(BF16)
    ulow[my_row] = (unit - u16.astype(F32)).astype(BF16)
    ucol[my_col] = u16
    urow[my_row] = u16
    my_lab = lab[...].astype(F32)
    lcol[my_col] = my_lab
    inv_lanes = jnp.transpose(jnp.broadcast_to(inv_norm, (ROWS, ROWS)))[0:1, :]
    lrow[my_row] = jnp.concatenate([my_lab, inv_lanes], axis=0)

    pl.semaphore_wait(barrier, len(peers))

    lab_p = {o: cp.send(lcol.at[my_col], lcol.at[my_col], p_dev[o]) for o in RING}
    lab_z = {o: cp.send(lrow.at[my_row], lrow.at[my_row], z_dev[o]) for o in RING}

    def col(o_p, o_q):
        return ring(q, o_q) * SIDE + ring(p, o_p)

    def row(o_z):
        return c * SIDE + ring(z, o_z)

    def row_sib(o_z):
        return other * SIDE + ring(z, o_z)

    def spread(ref, slot, devs, offsets=RING):
        return {o: cp.send(ref.at[slot], ref.at[slot], devs[o]) for o in offsets}

    p_ids = spread(ucol, my_col, p_dev, (1, 3))
    first_sent, cp.started = cp.started[-2:], cp.started[:-2]
    z_ids = spread(urow, my_row, z_dev)
    sib_ids = {0: cp.send(urow.at[my_row], urow.at[my_row], sib)}
    for copy in first_sent:
        copy.wait_send()
    p_ids.update(spread(ucol, my_col, p_dev, (2,)))
    q_ids = {0: spread(ucol, my_col, q_dev, (1, 3))}
    late_z = [(ulow, spread(ulow, my_row, z_dev, (1, 3)))]

    turn = jnp.transpose(feat[...].astype(F32)).reshape(SIDE, SIDE, 2, SIDE, 8, ROWS)
    for z_ in range(SIDE):
        for x_ in range(SIDE):
            for c_ in range(2):
                for y_ in range(SIDE):
                    feat_t[c_, x_, y_, z_] = turn[z_, x_, c_, y_]
    frow[my_row] = feat_t[...].reshape(FEATURES, ROWS).astype(BF16)
    late_z.append((frow, spread(frow, my_row, z_dev, (1, 3))))

    for o in RING:
        cp.arrived(lcol.at[col(SIDE - o, 0)], lab_p[o])
        cp.arrived(lrow.at[row(SIDE - o)], lab_z[o])
    my_line = lcol.at[pl.ds(q * SIDE, SIDE)]
    lab_q = {o: cp.send(my_line, my_line, q_dev[o]) for o in RING}
    my_set = lrow.at[pl.ds(c * SIDE, SIDE)]
    lab_s = cp.send(my_set, my_set, sib)

    for o in (1, 3):
        back = SIDE - o
        cp.arrived(ucol.at[col(back, 0)], p_ids[o])
        q_ids[back] = spread(ucol, col(back, 0), q_dev, (1, 3))
    cp.arrived(ucol.at[col(2, 0)], p_ids[2])
    q_ids[2] = spread(ucol, col(2, 0), q_dev, (1, 3))
    low, high = pl.ds(0, ROWS // 2), pl.ds(ROWS // 2, ROWS // 2)
    far_ids = {}

    def pass_on(o_p):
        before, after = col(o_p, 3), col(o_p, 1)
        cp.arrived(ucol.at[before], q_ids[o_p][1])
        up = cp.send(ucol.at[before, low], ucol.at[before, low], q_dev[1])
        cp.arrived(ucol.at[after], q_ids[o_p][3])
        down = cp.send(ucol.at[after, high], ucol.at[after, high], q_dev[3])
        far_ids[o_p] = (up, down)

    for o in RING:
        back = SIDE - o
        cp.arrived(urow.at[row(back)], z_ids[o])
        sib_ids[back] = cp.send(urow.at[row(back)], urow.at[row(back)], sib)

    late_s = [(ref, {0: cp.send(ref.at[my_row], ref.at[my_row], sib)}) for ref in (ulow, frow)]

    for o in RING:
        line = lcol.at[pl.ds(ring(q, SIDE - o) * SIDE, SIDE)]
        cp.arrived(line, lab_q[o])
    cp.arrived(lrow.at[pl.ds(other * SIDE, SIDE)], lab_s)

    pass_on(0)

    lane = lax.broadcasted_iota(jnp.int32, (ROWS, ROWS), 1)

    def turned(block):
        pad = jnp.zeros((ROWS - block.shape[0], ROWS), F32)
        return jnp.transpose(jnp.concatenate([block, pad], axis=0))

    lab_t = turned(jnp.concatenate([lrow[k] for k in range(ROW_BLOCKS)], axis=0))
    for k in range(ROW_BLOCKS):
        rlab[k * ROWS : (k + 1) * ROWS, :] = lab_t[:, 2 * k : 2 * k + 1]
        rnorm[k * ROWS : (k + 1) * ROWS, :] = lab_t[:, 2 * k + 1 : 2 * k + 2] * INV_SHARPNESS

    def count_block(k, carry):
        rows = pl.ds(pl.multiple_of(k * ROWS, ROWS), ROWS)
        mine = rlab[rows, :]
        total = jnp.zeros((ROWS, ROWS), F32)
        for j in range(COL_BLOCKS):
            total = total + jnp.where(mine == lcol[j], 1.0, 0.0)
        rcnt[rows, :] = jnp.sum(total, axis=1, keepdims=True)
        racc[rows, :] = jnp.zeros((ROWS, ROWS), F32)
        return carry

    lax.fori_loop(0, ROW_BLOCKS, count_block, 0)
    pass_on(3)
    pass_on(1)

    for o in (0, 3, 1, 2):
        cp.arrived(urow.at[row_sib(o)], sib_ids[o])

    TILE = 256

    def line_tiles(q_, own_line):
        keys = ucol[pl.ds(q_ * SIDE, SIDE)].reshape(LINE, WIDTH)
        queries = urow[...].reshape(ROW_BLOCKS * ROWS, WIDTH)
        value = jnp.exp2(dot_nt(queries, keys) * LOG2_SCALE)
        if own_line:
            i = lax.broadcasted_iota(jnp.int32, value.shape, 0) - my_row * ROWS
            j = lax.broadcasted_iota(jnp.int32, value.shape, 1) - p * ROWS
            value = jnp.where((i == j) & (j >= 0) & (j < ROWS), 0.0, value)
        e[q_] = value
        racc[...] += (
            value[:, 0:ROWS]
            + value[:, ROWS : 2 * ROWS]
            + value[:, 2 * ROWS : 3 * ROWS]
            + value[:, 3 * ROWS : 4 * ROWS]
        )
        return jnp.sum(value.reshape(ROW_BLOCKS * ROWS // 8, 8, LINE), axis=0)

    def put_sums(q_, sums):
        total = jnp.sum(sums, axis=0, keepdims=True)
        for k in range(SIDE):
            csum[pl.ds(q_ * SIDE + k, 1), :] = total[:, k * ROWS : (k + 1) * ROWS]

    put_sums(q, line_tiles(q, True))

    def ref_halves(ref):
        n = ref.shape[1] // 2
        return pl.ds(0, n), pl.ds(n, n)

    pass_on(2)
    late_far = []
    for (ref, z_sent), (_, s_sent) in zip(late_z, late_s):
        low_part, high_part = ref_halves(ref)
        before, after = row(3), row(1)
        cp.arrived(ref.at[before], z_sent[1])
        up = cp.send(ref.at[before, low_part], ref.at[before, low_part], z_dev[1])
        s_sent[3] = cp.send(ref.at[before], ref.at[before], sib)
        cp.arrived(ref.at[after], z_sent[3])
        down = cp.send(ref.at[after, high_part], ref.at[after, high_part], z_dev[3])
        s_sent[1] = cp.send(ref.at[after], ref.at[after], sib)
        late_far.append((up, down))

    for o in RING:
        if o == 2:
            for o_p in (0, 3, 1, 2):
                far = col(o_p, 2)
                cp.arrived(ucol.at[far, low], far_ids[o_p][0])
                cp.arrived(ucol.at[far, high], far_ids[o_p][1])
        q_ = ring(q, SIDE - o)
        put_sums(q_, line_tiles(q_, False))

    c_ids = {o: cp.send(csum, cz.at[o[0] * SIDE + o[1]], plane[o]) for o in PLANE}
    table = jnp.zeros((ROWS, ROWS), F32)
    for k in range(ROW_BLOCKS):
        rows = slice(k * ROWS, (k + 1) * ROWS)
        table = jnp.where(lane == k, jnp.sum(racc[rows, :], axis=1, keepdims=True), table)
        table = jnp.where(lane == ROW_BLOCKS + k, rcnt[rows, :], table)
    trow[...] = jnp.transpose(table)[0 : 2 * ROW_BLOCKS, :]
    t_ids = {}
    for o in RING:
        t_ids[o] = cp.send(trow, tz.at[o], z_dev[o])
        t_ids[4 + o] = cp.send(trow, tz.at[4 + o], z_sib[o])
    t_ids[4] = cp.send(trow, tz.at[4], sib)

    lab_lanes = jnp.concatenate([lcol[j] for j in range(COL_BLOCKS)], axis=1)

    def all_keys():
        return ucol[...].reshape(COL_BLOCKS * ROWS, WIDTH)

    def class_tile(r, carry):
        rows = pl.ds(pl.multiple_of(r * TILE, TILE), TILE)
        same = jnp.where(rlab[rows, :] == lab_lanes, 1.0, 0.0).astype(BF16)
        mu[rows, :] = dot(same, all_keys())
        return carry

    lax.fori_loop(0, 4, class_tile, 0)
    my_rows = pl.ds(pl.multiple_of(my_row * ROWS, ROWS), ROWS)
    mu[my_rows, :] = mu[my_rows, :] - urow[my_row].astype(F32)

    rho = lax.broadcasted_iota(jnp.int32, (8 * ROW_BLOCKS, 1), 0)
    block, k_slot = rho // 8, rho % 8
    owner = (((block % SIDE) * SIDE + x) * 2 + block // SIDE) * SIDE + y
    wanted = jnp.where(k_slot < 4, owner * 4 + k_slot, -1)
    class_of = jnp.zeros((8 * ROW_BLOCKS, ROWS), F32)
    lane_row = lax.broadcasted_iota(jnp.int32, (8 * ROW_BLOCKS, ROWS), 1)
    for j in range(CLASSES // ROWS):
        hit = slots[j : j + 1, :] == wanted
        class_of = class_of + jnp.where(hit, (lane_row + (j * ROWS + 1)).astype(F32), 0.0)
    class_of = jnp.sum(class_of, axis=1, keepdims=True) - 1.0
    member = jnp.where(class_of == lab_lanes, 1.0, 0.0).astype(BF16)
    s_part[...] = dot(member, all_keys()).reshape(2, SIDE, 8, WIDTH)
    s_id = cp.send(s_part.at[other], s_recv, sib)

    totals = trow[...]
    for o in t_ids:
        cp.arrived(tz.at[o], t_ids[o])
        totals = totals + tz[o]
    first = lax.broadcasted_iota(jnp.int32, (2 * ROW_BLOCKS, ROWS), 0) < ROW_BLOCKS
    scales = turned(1.0 / jnp.where(first, totals, jnp.maximum(totals - 1.0, 1.0)))
    for k in range(ROW_BLOCKS):
        rows = slice(k * ROWS, (k + 1) * ROWS)
        rinv[rows, :] = scales[:, k : k + 1]
        pinv[rows, :] = 2.0 * scales[:, ROW_BLOCKS + k : ROW_BLOCKS + k + 1]
    col_totals = csum[...]
    for o in PLANE:
        cp.arrived(cz.at[o[0] * SIDE + o[1]], c_ids[o])
        col_totals = col_totals + cz[o[0] * SIDE + o[1]]
    for (ref, s_sent), (up, down) in zip(late_s, late_far):
        low_part, high_part = ref_halves(ref)
        cp.arrived(ref.at[row(2), low_part], up)
        cp.arrived(ref.at[row(2), high_part], down)
        s_sent[2] = cp.send(ref.at[row(2)], ref.at[row(2)], sib)
    cp.finish()
    cinv = 1.0 / col_totals
    cinv_lines = [
        jnp.concatenate([cinv[l * SIDE + k : l * SIDE + k + 1, :] for k in range(SIDE)], axis=1)
        for l in range(SIDE)
    ]

    def gradient(rows):
        scale = rinv[rows, :]
        weights = jnp.concatenate(
            [(e[l, rows, :] * (scale + cinv_lines[l])).astype(BF16) for l in range(SIDE)], axis=1
        )
        return dot(weights, all_keys()) - pinv[rows, :] * mu[rows, :]

    def project(part, rows, block, count):
        high = urow[pl.ds(block, count)].astype(F32).reshape(part.shape)
        unit = high + ulow[pl.ds(block, count)].astype(F32).reshape(part.shape)
        radial = jnp.sum(unit * part, axis=1, keepdims=True)
        return (rnorm[rows, :] * (part - unit * radial)).astype(BF16)

    def late_wait(o):
        for ref, s_sent in late_s:
            cp.arrived(ref.at[row_sib(o)], s_sent[o])

    for c_, keep in ((other, osib), (c, obuf)):
        rows = pl.ds(pl.multiple_of(c_ * LINE, LINE), LINE)
        part = gradient(rows)
        keep[...] = part
        if keep is osib:
            o_id = cp.send(osib, orecv, sib)
        if keep is osib:
            for o in range(SIDE):
                late_wait(o)
        dpart[rows, :] = project(part, rows, c_ * SIDE, SIDE)

    def feats(c_, h):
        runs = pl.ds(pl.multiple_of(c_ * LINE + h * TILE, TILE), TILE)
        return jnp.concatenate([frow[k, runs, :] for k in range(ROW_BLOCKS)], axis=1)

    gs_ids = []
    for h in range(2):
        half = pl.ds(h * TILE, TILE)
        g_sib[half] = dot(feats(other, h), dpart[...])
        gs_ids.append(cp.send(g_sib.at[half], g_sib_recv.at[half], sib))
    for h in range(2):
        g_own[pl.ds(2 * h, 2)] = dot(feats(c, h), dpart[...]).reshape(2, SIDE, 4 * 8, WIDTH)

    cp.arrived(s_recv, s_id)
    s_recv[...] = s_recv[...] + s_part[c]
    s_ids = [cp.send(s_recv.at[ring(z, o)], s_zrecv.at[o - 1], z_dev[o]) for o in (1, 2, 3)]

    o_zids = {}
    cp.arrived(orecv, o_id)

    def rows_of(z_):
        there = pl.ds(pl.multiple_of(z_ * ROWS, ROWS), ROWS)
        return obuf[there, :] + orecv[there, :]

    for o in (2, 1, 3):
        zsend[o - 1] = rows_of(ring(z, o)).astype(BF16)
        o_zids[o] = cp.send(zsend.at[o - 1], zrecv.at[o - 1], z_dev[o])

    for h in range(2):
        cp.arrived(g_sib_recv.at[pl.ds(h * TILE, TILE)], gs_ids[h])

    def g_rows(x_, y_):
        runs = pl.ds(pl.multiple_of((x_ * SIDE + y_) * 32, 32), 32)
        return g_own[x_, y_] + g_sib_recv[runs, :]

    g_ids = {}
    for o in PLANE:
        k = o[0] * SIDE + o[1]
        g_send[k] = g_rows(ring(x, o[0]), ring(y, o[1])).astype(BF16)
        g_ids[o] = cp.send(g_send.at[k], g_recv.at[k], plane[o])

    for o in (1, 2, 3):
        cp.arrived(s_zrecv.at[o - 1], s_ids[o - 1])
    own_out[...] = (s_recv[z] + s_zrecv[0] + s_zrecv[1] + s_zrecv[2])[0:4, :]
    part = rows_of(z)
    for o in (1, 3, 2):
        cp.arrived(zrecv.at[o - 1], o_zids[o])
        part = part + zrecv[o - 1].astype(F32)
    pg_out[...] = project(part, my_rows, my_row, 1)

    part = g_rows(x, y)
    for o in PLANE[::-1]:
        k = o[0] * SIDE + o[1]
        cp.arrived(g_recv.at[k], g_ids[o])
        part = part + g_recv[k].astype(F32)
    g_zsend[...] = part.reshape(SIDE, 8, WIDTH)
    ids = {o: cp.send(g_zsend.at[ring(z, o)], g_zrecv.at[o - 1], z_dev[o]) for o in (2, 1, 3)}
    cp.finish(3)
    part = g_zsend[z]
    for o in (1, 3, 2):
        cp.arrived(g_zrecv.at[o - 1], ids[o])
        part = part + g_zrecv[o - 1]
    wg_out[...] = part

    cp.finish()


def body(features, proj_weight, labels, owner_slot):
    vmem = pl.BlockSpec(memory_space=pltpu.VMEM)
    rows_all = ROW_BLOCKS * ROWS
    scratch = [
        pltpu.VMEM((ROWS, FEATURES), BF16),
        pltpu.VMEM((FEATURES, WIDTH), BF16),
        pltpu.VMEM((1, ROWS), jnp.int32),
        pltpu.VMEM((CLASSES // ROWS, ROWS), jnp.int32),
        pltpu.VMEM((COL_BLOCKS, ROWS, WIDTH), BF16),
        pltpu.VMEM((ROW_BLOCKS, ROWS, WIDTH), BF16),
        pltpu.VMEM((ROW_BLOCKS, ROWS, WIDTH), BF16),
        pltpu.VMEM((ROW_BLOCKS, FEATURES, ROWS), BF16),
        pltpu.VMEM((2, SIDE, SIDE, SIDE, 8, ROWS), F32),
        pltpu.VMEM((SIDE, rows_all, LINE), F32),
        pltpu.VMEM((COL_BLOCKS, 1, ROWS), F32),
        pltpu.VMEM((ROW_BLOCKS, 2, ROWS), F32),
        pltpu.VMEM((rows_all, 1), F32),
        pltpu.VMEM((rows_all, 1), F32),
        pltpu.VMEM((rows_all, ROWS), F32),
        pltpu.VMEM((rows_all, 1), F32),
        pltpu.VMEM((rows_all, 1), F32),
        pltpu.VMEM((rows_all, 1), F32),
        pltpu.VMEM((COL_BLOCKS, ROWS), F32),
        pltpu.VMEM((16, COL_BLOCKS, ROWS), F32),
        pltpu.VMEM((2 * ROW_BLOCKS, ROWS), F32),
        pltpu.VMEM((8, 2 * ROW_BLOCKS, ROWS), F32),
        pltpu.VMEM((rows_all, WIDTH), F32),
        pltpu.VMEM((LINE, WIDTH), F32),
        pltpu.VMEM((LINE, WIDTH), F32),
        pltpu.VMEM((LINE, WIDTH), F32),
        pltpu.VMEM((rows_all, WIDTH), BF16),
        pltpu.VMEM((LINE, WIDTH), F32),
        pltpu.VMEM((LINE, WIDTH), F32),
        pltpu.VMEM((3, ROWS, WIDTH), BF16),
        pltpu.VMEM((3, ROWS, WIDTH), BF16),
        pltpu.VMEM((SIDE, SIDE, 4 * 8, WIDTH), F32),
        pltpu.VMEM((16, 4 * 8, WIDTH), BF16),
        pltpu.VMEM((16, 4 * 8, WIDTH), BF16),
        pltpu.VMEM((SIDE, 8, WIDTH), F32),
        pltpu.VMEM((3, 8, WIDTH), F32),
        pltpu.VMEM((2, SIDE, 8, WIDTH), F32),
        pltpu.VMEM((SIDE, 8, WIDTH), F32),
        pltpu.VMEM((3, 8, WIDTH), F32),
        pltpu.SemaphoreType.DMA((N_COPIES,)),
        pltpu.SemaphoreType.DMA((N_COPIES,)),
        pltpu.SemaphoreType.DMA((4,)),
    ]
    return pl.pallas_call(
        kernel,
        out_shape=(
            pltpu.VMEM((ROWS, WIDTH), BF16),
            pltpu.VMEM((8, WIDTH), F32),
            pltpu.VMEM((4, WIDTH), F32),
        ),
        in_specs=[pl.BlockSpec(memory_space=pl.ANY)] * 4,
        out_specs=(vmem,) * 3,
        scratch_shapes=scratch,
        compiler_params=pltpu.CompilerParams(
            collective_id=0, has_side_effects=True, vmem_limit_bytes=56 * 1024 * 1024
        ),
        name="contrastive",
    )(features, proj_weight, labels.reshape(1, ROWS), owner_slot.reshape(CLASSES // ROWS, ROWS))


def solution(mesh):
    in_specs = (P(("dp", "grp"), None), P(), P(("dp", "grp")), P())
    out_specs = (P(("dp", "grp"), None), P(("dp", "grp"), None), P(("dp", "grp"), None))
    return jax.shard_map(body, mesh=mesh, in_specs=in_specs, out_specs=out_specs, check_vma=False)
```
